32 devices in a mesh: seq: 8 (over z, y), tp: 4 (over x, core).
Axes of the slice: x: 2, y: 2, z: 4, core: 2. Of those that a mesh axis runs over, the one named last changes fastest.
Arguments:
- image_rows: bfloat16 [1024, 1280], P('seq'), may hold values from -6 to 6
- norm_gain: float32 [1280], replicated, may hold values from 0.1 to 1.9
- expand_weight: bfloat16 [1280, 5120], P(None, 'tp'), may hold values from -0.15625 to 0.15625
- shrink_weight: bfloat16 [5120, 1280], P('tp'), may hold values from -0.078125 to 0.078125
- projector: bfloat16 [1280, 8192], P(None, 'tp'), may hold values from -0.15625 to 0.15625
- kv_weight: bfloat16 [8192, 2048], P('tp', 'seq'), may hold values from -0.0625 to 0.0625
- queries: bfloat16 [2048, 8192], P('seq', 'tp'), may hold values from -240 to 240
- send_list: int32 [8, 8, 32], P('seq'), may hold values from -1 to 127, as said below
- block_mask: int32 [16, 4], P('seq'), may hold values from 0 to 1, as said below
Outputs:
- states: bfloat16 [1024, 8192], P('seq', 'tp')
- context: bfloat16 [2048, 8192], P('seq', 'tp')
The draws below stay inside these ranges and needn't reach their ends.
Inputs may be any that keep to these rules, and one draw needn't show every extreme that they name: `send_list`: each sequence shard belongs to one document, whose text fills a run of whole sequence shards, and references that document's one image of 1 to 4 tiles; each draw has a document of one tile and one of 4. The image's 32 rows on encoder shard s form a run of consecutive local rows, named in order and alike for every sequence shard of the document; slot s * 32 + c is live exactly when it is below 64 times the image's tile count, else -1. block_mask[b, q] is 1 exactly when tile q is among the tiles of the image of block b's document and block b does not precede that image; at most the first block of a document precedes it. So a seen slot is always live.
All inputs are finite; a program needn't handle non-finite values.
Results may differ from the reference program's by a relative error of at most 0.03.
Values may be sent and summed in bfloat16 or wider, within the bound.
A program may use at most 64 MiB of HBM per device.

```python
import math
import jax
import jax.numpy as jnp
from jax import lax

VIT_D = 1280
VIT_FF = 5120
D = 8192
HEADS = 64
KV_HEADS = 8
HDIM = 128
MAX_TILES = 4
IMG_DEV = 128
TOK_DEV = 256
SLOTS_DEV = 256
QBLK = 128
CAP = 32
TILE_ROWS = 64
IMAGES = 4
TOKENS = 2048
IMG_ROWS = 1024
N_SEQ = 8


def shuffled_images(sub_key):
    return jax.random.permutation(sub_key, IMAGES).astype(jnp.int32)


def document_layout(key):
    base_key = jax.random.fold_in(key, 101)
    cut_key, count_key, pick_key, order_key, offset_key = jax.random.split(base_key, 5)
    boundaries = jax.random.permutation(cut_key, N_SEQ - 1)[:IMAGES - 1].astype(jnp.int32) + 1
    shard_ids = jnp.arange(N_SEQ, dtype=jnp.int32)
    shard_document = jnp.sum((boundaries[None, :] <= shard_ids[:, None]).astype(jnp.int32), axis=1)
    first_shard = jnp.concatenate([jnp.zeros((1,), jnp.int32), jnp.sort(boundaries)])
    document_ids = jnp.arange(IMAGES, dtype=jnp.int32)
    document_shards = jnp.sum((shard_document[None, :] == document_ids[:, None]).astype(jnp.int32), axis=1)
    tile_counts = jax.random.randint(count_key, (IMAGES,), 1, MAX_TILES + 1, dtype=jnp.int32)
    forced = jax.random.permutation(pick_key, IMAGES)
    tile_counts = tile_counts.at[forced[0]].set(1).at[forced[1]].set(MAX_TILES)
    run_orders = jax.vmap(shuffled_images)(jax.random.split(order_key, N_SEQ))
    blocks_dev = TOK_DEV // QBLK
    offset_draw = jax.random.randint(offset_key, (IMAGES,), 0, 2, dtype=jnp.int32)
    image_offset = jnp.minimum(offset_draw, document_shards * blocks_dev - 1)
    return (shard_document, tile_counts, run_orders, first_shard, image_offset)


def draw_send_list(key, part):
    shard_document, tile_counts, run_orders, first_shard, image_offset = document_layout(key)
    source = jnp.arange(N_SEQ, dtype=jnp.int32)[:, None, None]
    column = jnp.arange(CAP, dtype=jnp.int32)[None, None, :]
    position = run_orders[:, shard_document]
    local_row = position[:, :, None] * CAP + column
    live_limit = (tile_counts[shard_document] * TILE_ROWS)[None, :, None]
    live = source * CAP + column < live_limit
    return jnp.where(live, local_row, -1).astype(jnp.int32)


def draw_block_mask(key, part):
    shard_document, tile_counts, run_orders, first_shard, image_offset = document_layout(key)
    blocks_dev = TOK_DEV // QBLK
    block_ids = jnp.arange(N_SEQ * blocks_dev, dtype=jnp.int32)
    block_document = shard_document[block_ids // blocks_dev]
    image_block = first_shard[block_document] * blocks_dev + image_offset[block_document]
    after_image = block_ids >= image_block
    tile_ids = jnp.arange(MAX_TILES, dtype=jnp.int32)
    tile_live = tile_ids[None, :] < tile_counts[block_document][:, None]
    return (after_image[:, None] & tile_live).astype(jnp.int32)


def draw_queries(key, part):
    value_key = jax.random.fold_in(jax.random.fold_in(key, 23), 0)
    full_shape = (TOKENS, HEADS * HDIM)
    normal_draw = jnp.clip(jax.random.normal(value_key, full_shape, jnp.float32), -6.0, 6.0)
    return (normal_draw * 1.5).astype(jnp.bfloat16)


def level_of(key, extent, cuts, least, largest):
    def one(dim, parts):
        steps = jax.random.uniform(jax.random.fold_in(jax.random.fold_in(key, 6), dim), (parts,), jnp.float32, least / len(cuts), largest / len(cuts))
        return jnp.repeat(jnp.exp(steps), extent[dim] // parts).reshape((-1,) + (1,) * (len(extent) - dim - 1))

    level = one(*cuts[0])
    for cut in cuts[1:]:
        level = level * one(*cut)
    return level


def normal_values(own_key, extent, deviation, most, pieces=(), held_as=jnp.bfloat16):
    result = deviation * jax.random.normal(own_key, extent, jnp.float32)
    if pieces:
        result = result * level_of(own_key, extent, pieces, -0.22, 0.18)
    return jnp.clip(result, -most, most).astype(held_as)


def setup_inputs(seed: int = 0) -> dict:
    arg_keys = jax.random.split(jax.random.key(seed), 10)
    return {
        "image_rows": normal_values(arg_keys[0], (IMG_ROWS, VIT_D), 1.0, 6.0, ((0, 8),)),
        "norm_gain": jnp.clip(1.0 + 0.18 * jax.random.normal(arg_keys[1], (VIT_D,), jnp.float32), 0.1, 1.9),
        "expand_weight": normal_values(arg_keys[2], (VIT_D, VIT_FF), VIT_D ** -0.5, 0.15625, ((1, 4),)),
        "shrink_weight": normal_values(arg_keys[3], (VIT_FF, VIT_D), VIT_FF ** -0.5, 0.078125, ((0, 4),)),
        "projector": normal_values(arg_keys[4], (VIT_D, D), VIT_D ** -0.5, 0.15625, ((1, 4),)),
        "kv_weight": normal_values(arg_keys[5], (D, 2 * KV_HEADS * HDIM), D ** -0.5, 0.0625, ((0, 4), (1, 8))),
        "queries": draw_queries(jax.random.fold_in(arg_keys[9], 71), 0),
        "send_list": draw_send_list(jax.random.fold_in(arg_keys[9], 71), 0),
        "block_mask": draw_block_mask(jax.random.fold_in(arg_keys[9], 71), 0),
    }


def layer_norm(row_data, norm_gain):
    values = row_data.astype(jnp.float32)
    center = values - lax.optimization_barrier(jnp.mean(values, axis=1, keepdims=True))
    spread = lax.optimization_barrier(jnp.mean(center * center, axis=1, keepdims=True))
    return (center * lax.rsqrt(spread + 1e-05) * norm_gain).astype(jnp.bfloat16)

def attend(query_rows, key_rows, value_rows, visible):
    inverse_root = 1.0 / math.sqrt(query_rows.shape[3])
    scores = jnp.einsum('tkgd,skd->ktgs', query_rows, key_rows) * inverse_root
    mask_full = visible[None, :, None, :]
    masked = jnp.where(mask_full, scores, -jnp.inf)
    any_live = jnp.any(mask_full, axis=3, keepdims=True)
    row_max = jnp.where(any_live, lax.optimization_barrier(jnp.max(masked, axis=3, keepdims=True)), 0.0)
    weights = jnp.where(mask_full, jnp.exp(scores - row_max), 0.0)
    summed = jnp.where(any_live, lax.optimization_barrier(jnp.sum(weights, axis=3, keepdims=True)), 1.0)
    normalized = (weights / summed).astype(jnp.bfloat16)
    context = jnp.einsum('ktgs,skd->tkgd', normalized.astype(jnp.float32), value_rows)
    return context.reshape(query_rows.shape[0], -1).astype(jnp.bfloat16)

def reference(image_rows, norm_gain, expand_weight, shrink_weight, projector, kv_weight, queries, send_list, block_mask):
    normed = layer_norm(image_rows, norm_gain)
    hidden = jax.nn.gelu(jnp.dot(normed, expand_weight, preferred_element_type=jnp.float32), approximate=False).astype(jnp.bfloat16)
    vit_out = (image_rows.astype(jnp.float32) + jnp.dot(hidden, shrink_weight, preferred_element_type=jnp.float32)).astype(jnp.bfloat16)
    states = jnp.dot(vit_out, projector, preferred_element_type=jnp.float32).astype(jnp.bfloat16)
    kv_all = jnp.dot(states, kv_weight, preferred_element_type=jnp.float32).astype(jnp.bfloat16)
    group_size = HEADS // KV_HEADS
    row_bases = (jnp.arange(N_SEQ, dtype=jnp.int32) * IMG_DEV)[:, None]
    mask_rows_dev = TOK_DEV // QBLK
    slot_tile = jnp.arange(SLOTS_DEV, dtype=jnp.int32) // TILE_ROWS

    def one_target(target):
        slot_index = lax.dynamic_index_in_dim(send_list, target, 1, keepdims=False)
        global_rows = (row_bases + jnp.maximum(slot_index, 0)).reshape(-1).astype(jnp.int32)
        paired = jnp.take(kv_all, global_rows, axis=0).astype(jnp.float32).reshape(SLOTS_DEV, KV_HEADS, 2, HDIM)
        key_rows = paired[:, :, 0, :]
        value_rows = paired[:, :, 1, :]
        query_rows = lax.dynamic_slice_in_dim(queries, (target * TOK_DEV).astype(jnp.int32), TOK_DEV, 0)
        query_rows = query_rows.astype(jnp.float32).reshape(TOK_DEV, KV_HEADS, group_size, HDIM)
        mask_rows = lax.dynamic_slice_in_dim(block_mask, (target * mask_rows_dev).astype(jnp.int32), mask_rows_dev, 0)
        visible = jnp.take(mask_rows > 0, slot_tile, axis=1)
        visible = jnp.repeat(visible, QBLK, axis=0)
        return attend(query_rows, key_rows, value_rows, visible)
    per_target = lax.map(one_target, jnp.arange(N_SEQ, dtype=jnp.int32))
    return (states, per_target.reshape(TOKENS, HEADS * HDIM))
```

```python
import math

import jax
import jax.numpy as jnp
from jax import lax
from jax.experimental import pallas as pl
from jax.experimental.pallas import tpu as pltpu
from jax.sharding import PartitionSpec as P

HDIM = 128
MAX_TILES = 4
QBLK = 128


def layer_norm(row_data, norm_gain):
    values = row_data.astype(jnp.float32)
    center = values - jnp.mean(values, axis=1, keepdims=True)
    spread = jnp.mean(center * center, axis=1, keepdims=True)
    return (center * lax.rsqrt(spread + 1e-05) * norm_gain).astype(jnp.bfloat16)


def select_rows(row_data, wanted):
    flat = wanted.reshape(-1)
    hot = (flat[:, None] == jnp.arange(row_data.shape[0], dtype=jnp.int32)[None, :]).astype(jnp.bfloat16)
    picked = jnp.dot(hot, row_data, preferred_element_type=jnp.float32).astype(jnp.bfloat16)
    return picked.reshape(wanted.shape + (row_data.shape[1],))


def attend_kernel(mask_ref, q_ref, kv_ref, o_ref):
    tokens, width = q_ref.shape
    slots = kv_ref.shape[0]
    groups = kv_ref.shape[1] // (2 * HDIM)
    per_group = width // (groups * HDIM)
    tile_rows = slots // MAX_TILES
    scale = 1.0 / math.sqrt(HDIM)
    blocks = mask_ref.shape[0]
    slot = lax.broadcasted_iota(jnp.int32, (QBLK, slots), 1)
    for b in range(blocks):
        seen = jnp.zeros((QBLK, slots), jnp.float32)
        for tile in range(MAX_TILES):
            inside = (slot >= tile * tile_rows) & (slot < (tile + 1) * tile_rows)
            seen = jnp.where(inside, (mask_ref[b, tile] > 0).astype(jnp.float32), seen)
        visible = seen > 0.0
        rows = pl.ds(b * QBLK, QBLK)
        for g in range(groups):
            key_rows = kv_ref[:, g * 2 * HDIM:g * 2 * HDIM + HDIM]
            value_rows = kv_ref[:, g * 2 * HDIM + HDIM:(g + 1) * 2 * HDIM]
            for h in range(per_group):
                cols = pl.ds((g * per_group + h) * HDIM, HDIM)
                scores = lax.dot_general(
                    q_ref[rows, cols], key_rows, (((1,), (1,)), ((), ())),
                    preferred_element_type=jnp.float32) * scale
                masked = jnp.where(visible, scores, -1e30)
                top = jnp.max(masked, axis=1, keepdims=True)
                weights = jnp.where(visible, jnp.exp(masked - top), 0.0)
                total = jnp.sum(weights, axis=1, keepdims=True)
                total = jnp.where(total > 0.0, total, 1.0)
                probs = (weights / total).astype(jnp.bfloat16)
                o_ref[rows, cols] = jnp.dot(
                    probs, value_rows, preferred_element_type=jnp.float32).astype(jnp.bfloat16)


def attend(queries, kv_slots, block_mask):
    tokens, width = queries.shape
    return pl.pallas_call(
        attend_kernel,
        out_shape=jax.ShapeDtypeStruct((tokens, width), jnp.bfloat16),
        in_specs=[
            pl.BlockSpec(memory_space=pltpu.SMEM),
            pl.BlockSpec(memory_space=pltpu.VMEM),
            pl.BlockSpec(memory_space=pltpu.VMEM),
        ],
        out_specs=pl.BlockSpec(memory_space=pltpu.VMEM),
        cost_estimate=pl.CostEstimate(
            flops=4 * tokens * kv_slots.shape[0] * width, bytes_accessed=4 * tokens * width,
            transcendentals=tokens * kv_slots.shape[0] * width // HDIM),
        compiler_params=pltpu.CompilerParams(vmem_limit_bytes=24 * 1024 * 1024),
    )(block_mask, queries, kv_slots)


def local(
    image_rows,
    norm_gain,
    expand_weight,
    shrink_weight,
    projector,
    kv_weight,
    queries,
    send_list,
    block_mask,
):
    wanted = send_list[0]
    fold_part = jnp.dot(projector, kv_weight, preferred_element_type=jnp.float32).astype(jnp.bfloat16)
    fold_rows = lax.psum_scatter(fold_part, "tp", scatter_dimension=0, tiled=True)
    fold_rows = lax.all_gather(fold_rows, "seq", axis=1, tiled=True)
    normed = layer_norm(image_rows, norm_gain)
    hidden = jax.nn.gelu(
        jnp.dot(normed, expand_weight, preferred_element_type=jnp.float32), approximate=False
    ).astype(jnp.bfloat16)
    partial_value = jnp.dot(hidden, shrink_weight, preferred_element_type=jnp.float32).astype(jnp.bfloat16)
    own_sum = lax.psum_scatter(partial_value, "tp", scatter_dimension=1, tiled=True)
    share_width = own_sum.shape[1]
    own_rows = lax.dynamic_slice_in_dim(
        image_rows, lax.axis_index("tp") * share_width, share_width, 1
    )
    own_share = (own_rows.astype(jnp.float32) + own_sum.astype(jnp.float32)).astype(jnp.bfloat16)
    vit_out = lax.all_gather(own_share, "tp", axis=1, tiled=True)
    states = jnp.dot(vit_out, projector, preferred_element_type=jnp.float32).astype(jnp.bfloat16)
    outgoing = select_rows(own_share, wanted)
    arrived = lax.all_to_all(outgoing, "seq", split_axis=0, concat_axis=0, tiled=True)
    slot_rows = arrived.reshape(-1, share_width)
    kv_part = jnp.dot(slot_rows, fold_rows, preferred_element_type=jnp.float32).astype(jnp.bfloat16)
    kv_slots = lax.psum_scatter(kv_part, "tp", scatter_dimension=1, tiled=True)
    return (states, attend(queries, kv_slots, block_mask))


def solution(mesh):
    placed = (
        P("seq", None),
        P(),
        P(None, "tp"),
        P("tp", None),
        P(None, "tp"),
        P("tp", "seq"),
        P("seq", "tp"),
        P("seq", None, None),
        P("seq", None),
    )
    return jax.shard_map(
        local,
        mesh=mesh,
        in_specs=placed,
        out_specs=(P("seq", "tp"), P("seq", "tp")),
        check_vma=False,
    )
```

```python
import functools
import math

import jax
import jax.numpy as jnp
from jax import lax
from jax.experimental import pallas as pl
from jax.experimental.pallas import tpu as pltpu
from jax.sharding import PartitionSpec as P

HDIM = 128
MAX_TILES = 4
QBLK = 128


def layer_norm(row_data, norm_gain):
    values = row_data.astype(jnp.float32)
    center = values - jnp.mean(values, axis=1, keepdims=True)
    spread = jnp.mean(center * center, axis=1, keepdims=True)
    return (center * lax.rsqrt(spread + 1e-05) * norm_gain).astype(jnp.bfloat16)


def select_rows(row_data, wanted):
    flat = wanted.reshape(-1)
    hot = (flat[:, None] == jnp.arange(row_data.shape[0], dtype=jnp.int32)[None, :]).astype(jnp.bfloat16)
    picked = jnp.dot(hot, row_data, preferred_element_type=jnp.float32).astype(jnp.bfloat16)
    return picked.reshape(wanted.shape + (row_data.shape[1],))


def attend_kernel(mask_ref, q_ref, kv_ref, o_ref):
    tokens, width = q_ref.shape
    slots = kv_ref.shape[0]
    groups = kv_ref.shape[1] // (2 * HDIM)
    per_group = width // (groups * HDIM)
    tile_rows = slots // MAX_TILES
    scale = 1.0 / math.sqrt(HDIM)
    blocks = mask_ref.shape[0]
    slot = lax.broadcasted_iota(jnp.int32, (QBLK, slots), 1)
    for b in range(blocks):
        seen = jnp.zeros((QBLK, slots), jnp.float32)
        for tile in range(MAX_TILES):
            inside = (slot >= tile * tile_rows) & (slot < (tile + 1) * tile_rows)
            seen = jnp.where(inside, (mask_ref[b, tile] > 0).astype(jnp.float32), seen)
        visible = seen > 0.0
        rows = pl.ds(b * QBLK, QBLK)
        for g in range(groups):
            key_rows = kv_ref[:, g * 2 * HDIM:g * 2 * HDIM + HDIM]
            value_rows = kv_ref[:, g * 2 * HDIM + HDIM:(g + 1) * 2 * HDIM]
            for h in range(per_group):
                cols = pl.ds((g * per_group + h) * HDIM, HDIM)
                scores = lax.dot_general(
                    q_ref[rows, cols], key_rows, (((1,), (1,)), ((), ())),
                    preferred_element_type=jnp.float32) * scale
                masked = jnp.where(visible, scores, -1e30)
                top = jnp.max(masked, axis=1, keepdims=True)
                weights = jnp.where(visible, jnp.exp(masked - top), 0.0)
                total = jnp.sum(weights, axis=1, keepdims=True)
                total = jnp.where(total > 0.0, total, 1.0)
                probs = (weights / total).astype(jnp.bfloat16)
                o_ref[rows, cols] = jnp.dot(
                    probs, value_rows, preferred_element_type=jnp.float32).astype(jnp.bfloat16)


def attend(queries, kv_slots, block_mask):
    tokens, width = queries.shape
    return pl.pallas_call(
        attend_kernel,
        out_shape=jax.ShapeDtypeStruct((tokens, width), jnp.bfloat16),
        in_specs=[
            pl.BlockSpec(memory_space=pltpu.SMEM),
            pl.BlockSpec(memory_space=pltpu.VMEM),
            pl.BlockSpec(memory_space=pltpu.VMEM),
        ],
        out_specs=pl.BlockSpec(memory_space=pltpu.VMEM),
        cost_estimate=pl.CostEstimate(
            flops=4 * tokens * kv_slots.shape[0] * width, bytes_accessed=4 * tokens * width,
            transcendentals=tokens * kv_slots.shape[0] * width // HDIM),
        compiler_params=pltpu.CompilerParams(vmem_limit_bytes=24 * 1024 * 1024),
    )(block_mask, queries, kv_slots)


MESH = pl.DeviceIdType.MESH


def exchange_kernel(n_seq, n_tp, image_ref, gain_ref, expand_ref, shrink_ref, proj_ref, kvw_ref, hot_ref,
                    vit_ref, kv_ref,
                    fold_out, fold_in, gathered, mine, parts, parts_in, image_cut, chosen, slots,
                    a_s, a_r, b_s, b_r, g_r, up_s, down_s, y_s, x_s, m_r, v_s, v_r, s_s, s_r, f_s, f_r):
    s = lax.axis_index("seq")
    t = lax.axis_index("tp")
    z, y = s // 2, s % 2
    depth = proj_ref.shape[0] // n_tp
    cap = hot_ref.shape[0] // n_seq

    barrier = pltpu.get_barrier_semaphore()
    for j in range(1, n_tp):
        pl.semaphore_signal(barrier, inc=1, device_id=(s, lax.rem(t + j, n_tp)), device_id_type=MESH)
    for j in range(1, n_seq):
        pl.semaphore_signal(barrier, inc=1, device_id=(lax.rem(s + j, n_seq), t), device_id_type=MESH)

    def remote(src, dst, send, recv, where):
        return pltpu.make_async_remote_copy(src_ref=src, dst_ref=dst, send_sem=send, recv_sem=recv,
                                            device_id=where, device_id_type=MESH)

    sent = []

    def go(copy):
        copy.start()
        sent.append(copy)

    def fold_quarter(q):
        rows = pl.ds(pl.multiple_of(q * depth, 64), depth)
        return jnp.dot(proj_ref[rows, :], kvw_ref[...], preferred_element_type=jnp.float32)

    for j in range(1, n_tp):
        peer = lax.rem(t + j, n_tp)
        fold_out[j] = fold_quarter(peer).astype(jnp.bfloat16)
        if j == 1:
            pl.semaphore_wait(barrier, n_tp + n_seq - 2)
        go(remote(fold_out.at[j], fold_in.at[j], a_s.at[j], a_r.at[j], (s, peer)))
    own_fold = fold_quarter(t)

    values = image_ref[...].astype(jnp.float32)
    center = values - jnp.mean(values, axis=1, keepdims=True)
    spread = jnp.mean(center * center, axis=1, keepdims=True)
    normed = (center * lax.rsqrt(spread + 1e-05) * gain_ref[...]).astype(jnp.bfloat16)
    wide = jnp.dot(normed, expand_ref[...], preferred_element_type=jnp.float32)
    hidden = (0.5 * wide * (1.0 + lax.erf(wide * math.sqrt(0.5)))).astype(jnp.bfloat16)
    partial = jnp.dot(hidden, shrink_ref[...], preferred_element_type=jnp.float32)
    for q in range(n_tp):
        parts[q] = partial[:, q * depth:(q + 1) * depth].astype(jnp.bfloat16)
        image_cut[q] = values[:, q * depth:(q + 1) * depth]
    for j in range(1, n_tp):
        peer = lax.rem(t + j, n_tp)
        go(remote(parts.at[peer], parts_in.at[j], b_s.at[j], b_r.at[j], (s, peer)))

    def arrive(buf, sem):
        pltpu.make_async_copy(buf, buf, sem).wait()

    for j in range(1, n_tp):
        arrive(fold_in.at[j], a_r.at[j])
        own_fold += fold_in[j].astype(jnp.float32)
    gathered[s] = own_fold.astype(jnp.bfloat16)

    def up(zz):
        i = 2 * zz + y
        return remote(gathered.at[i], gathered.at[i], up_s.at[zz], g_r.at[i], (s + 2, t))

    def down(zz):
        i = 2 * zz + y
        return remote(gathered.at[i], gathered.at[i], down_s.at[zz], g_r.at[i], (s - 2, t))

    def across(zz):
        i = 2 * zz + y
        return remote(gathered.at[i], gathered.at[i], y_s.at[zz], g_r.at[i], (2 * z + 1 - y, t))

    def deliver(zz, yy):
        i = 2 * zz + yy
        return remote(gathered.at[i], mine.at[2 * t + yy], x_s.at[i], m_r.at[2 * t + yy], (s, zz))

    def hand_on(zz, yy):
        @pl.when(zz != t)
        def _():
            deliver(zz, yy).start()

        @pl.when(zz == t)
        def _():
            mine[2 * t + yy] = gathered[2 * zz + yy]

    @pl.when(z < n_tp - 1)
    def _():
        up(z).start()

    @pl.when(z > 0)
    def _():
        down(z).start()

    across(z).start()
    hand_on(z, y)

    share = parts[t].astype(jnp.float32)
    for j in range(1, n_tp):
        arrive(parts_in.at[j], b_r.at[j])
        share += parts_in[j].astype(jnp.float32)
    share = (image_cut[t] + share).astype(jnp.bfloat16)
    vit_ref[t] = share
    picked = jnp.dot(hot_ref[...], share, preferred_element_type=jnp.float32).astype(jnp.bfloat16)
    chosen[...] = picked.reshape(n_seq, cap, depth)
    slots[t, s] = chosen[s]
    for j in range(1, n_seq):
        peer = lax.rem(s + j, n_seq)
        go(remote(chosen.at[peer], slots.at[t, s], s_s.at[j], s_r.at[s], (peer, t)))
    for j in range(1, n_tp):
        go(remote(vit_ref.at[t], vit_ref.at[t], v_s.at[j], v_r.at[t], (s, lax.rem(t + j, n_tp))))

    def z_step(k):
        @pl.when(z - k >= 0)
        def _():
            arrive(gathered.at[2 * (z - k) + y], g_r.at[2 * (z - k) + y])

            @pl.when(z < n_tp - 1)
            def _():
                up(z - k).start()
            across(z - k).start()
            hand_on(z - k, y)

        @pl.when(z + k < n_tp)
        def _():
            arrive(gathered.at[2 * (z + k) + y], g_r.at[2 * (z + k) + y])

            @pl.when(z > 0)
            def _():
                down(z + k).start()
            across(z + k).start()
            hand_on(z + k, y)

    def y_step(zz):
        arrive(gathered.at[2 * zz + 1 - y], g_r.at[2 * zz + 1 - y])
        hand_on(zz, 1 - y)

    for j in range(1, n_seq):
        peer = lax.rem(s + j, n_seq)
        arrive(slots.at[t, peer], s_r.at[peer])
    for j in range(1, n_tp):
        go(remote(slots.at[t], slots.at[t], f_s.at[j], f_r.at[t], (s, lax.rem(t + j, n_tp))))
    z_step(1)
    y_step(z)
    for k in range(1, n_tp):
        if k > 1:
            z_step(k)

        @pl.when(z - k >= 0)
        def _():
            y_step(z - k)

        @pl.when(z + k < n_tp)
        def _():
            y_step(z + k)

    for j in range(1, n_tp):
        peer = lax.rem(t + j, n_tp)
        arrive(slots.at[peer], f_r.at[peer])
        arrive(vit_ref.at[peer], v_r.at[peer])
    for j in range(1, n_tp):
        peer = lax.rem(t + j, n_tp)
        for yy in range(2):
            arrive(mine.at[2 * peer + yy], m_r.at[2 * peer + yy])
    width = kvw_ref.shape[1]
    for yy in range(2):
        total = None
        for q in range(n_tp):
            term = jnp.dot(slots[q].reshape(n_seq * cap, depth), mine[2 * q + yy], preferred_element_type=jnp.float32)
            total = term if total is None else total + term
        kv_ref[:, yy * width:(yy + 1) * width] = total.astype(jnp.bfloat16)

    for copy in sent:
        copy.wait_send()
    for zz in range(n_tp):
        across(zz).wait_send()

        @pl.when((z < n_tp - 1) & (zz <= z))
        def _():
            up(zz).wait_send()

        @pl.when((z > 0) & (zz >= z))
        def _():
            down(zz).wait_send()

        @pl.when(zz != t)
        def _():
            for yy in range(2):
                deliver(zz, yy).wait_send()


def exchange(n_seq, n_tp, image_rows, norm_gain, expand_weight, shrink_weight, projector, kv_weight, hot):
    rows, features = image_rows.shape
    depth = features // n_tp
    width = kv_weight.shape[1]
    cap = hot.shape[0] // n_seq
    bf16, f32 = jnp.bfloat16, jnp.float32
    dma = pltpu.SemaphoreType.DMA
    vmem = pl.BlockSpec(memory_space=pltpu.VMEM)
    return pl.pallas_call(
        functools.partial(exchange_kernel, n_seq, n_tp),
        out_shape=(jax.ShapeDtypeStruct((n_tp, rows, depth), bf16),
                   jax.ShapeDtypeStruct((hot.shape[0], 2 * width), bf16)),
        in_specs=[vmem] * 7,
        out_specs=(vmem, vmem),
        scratch_shapes=[
            pltpu.VMEM((n_tp, depth, width), bf16),
            pltpu.VMEM((n_tp, depth, width), bf16),
            pltpu.VMEM((n_seq, depth, width), bf16),
            pltpu.VMEM((2 * n_tp, depth, width), bf16),
            pltpu.VMEM((n_tp, rows, depth), bf16),
            pltpu.VMEM((n_tp, rows, depth), bf16),
            pltpu.VMEM((n_tp, rows, depth), f32),
            pltpu.VMEM((n_seq, cap, depth), bf16),
            pltpu.VMEM((n_tp, n_seq, cap, depth), bf16),
            dma((n_tp,)), dma((n_tp,)), dma((n_tp,)), dma((n_tp,)),
            dma((n_seq,)), dma((n_tp,)), dma((n_tp,)), dma((n_tp,)), dma((n_seq,)), dma((2 * n_tp,)),
            dma((n_tp,)), dma((n_tp,)), dma((n_seq,)), dma((n_seq,)), dma((n_tp,)), dma((n_tp,)),
        ],
        compiler_params=pltpu.CompilerParams(
            collective_id=0, has_side_effects=True, vmem_limit_bytes=48 * 1024 * 1024),
    )(image_rows, norm_gain.reshape(1, -1), expand_weight, shrink_weight, projector, kv_weight, hot)


def local(
    image_rows,
    norm_gain,
    expand_weight,
    shrink_weight,
    projector,
    kv_weight,
    queries,
    send_list,
    block_mask,
):
    wanted = send_list[0]
    n_seq, n_tp = lax.axis_size("seq"), lax.axis_size("tp")
    if n_seq == 2 * n_tp and kv_weight.shape[1] == 2 * HDIM and wanted.shape[1] % 16 == 0:
        flat = wanted.reshape(-1)
        hot = (flat[:, None] == jnp.arange(image_rows.shape[0], dtype=jnp.int32)[None, :]).astype(jnp.bfloat16)
        shares, kv_slots = exchange(
            n_seq, n_tp, image_rows, norm_gain, expand_weight, shrink_weight, projector, kv_weight, hot)
        vit_out = jnp.transpose(shares, (1, 0, 2)).reshape(image_rows.shape)
        states = jnp.dot(vit_out, projector, preferred_element_type=jnp.float32).astype(jnp.bfloat16)
        return (states, attend(queries, kv_slots, block_mask))
    fold_part = jnp.dot(projector, kv_weight, preferred_element_type=jnp.float32).astype(jnp.bfloat16)
    fold_rows = lax.psum_scatter(fold_part, "tp", scatter_dimension=0, tiled=True)
    fold_rows = lax.all_gather(fold_rows, "seq", axis=1, tiled=True)
    normed = layer_norm(image_rows, norm_gain)
    hidden = jax.nn.gelu(
        jnp.dot(normed, expand_weight, preferred_element_type=jnp.float32), approximate=False
    ).astype(jnp.bfloat16)
    partial_value = jnp.dot(hidden, shrink_weight, preferred_element_type=jnp.float32).astype(jnp.bfloat16)
    own_sum = lax.psum_scatter(partial_value, "tp", scatter_dimension=1, tiled=True)
    share_width = own_sum.shape[1]
    own_rows = lax.dynamic_slice_in_dim(
        image_rows, lax.axis_index("tp") * share_width, share_width, 1
    )
    own_share = (own_rows.astype(jnp.float32) + own_sum.astype(jnp.float32)).astype(jnp.bfloat16)
    vit_out = lax.all_gather(own_share, "tp", axis=1, tiled=True)
    states = jnp.dot(vit_out, projector, preferred_element_type=jnp.float32).astype(jnp.bfloat16)
    outgoing = select_rows(own_share, wanted)
    arrived = lax.all_to_all(outgoing, "seq", split_axis=0, concat_axis=0, tiled=True)
    slot_rows = arrived.reshape(-1, share_width)
    kv_part = jnp.dot(slot_rows, fold_rows, preferred_element_type=jnp.float32).astype(jnp.bfloat16)
    kv_slots = lax.psum_scatter(kv_part, "tp", scatter_dimension=1, tiled=True)
    return (states, attend(queries, kv_slots, block_mask))


def solution(mesh):
    placed = (
        P("seq", None),
        P(),
        P(None, "tp"),
        P("tp", None),
        P(None, "tp"),
        P("tp", "seq"),
        P("seq", "tp"),
        P("seq", None, None),
        P("seq", None),
    )
    return jax.shard_map(
        local,
        mesh=mesh,
        in_specs=placed,
        out_specs=(P("seq", "tp"), P("seq", "tp")),
        check_vma=False,
    )
```

```python
import functools
import math

import jax
import jax.numpy as jnp
from jax import lax
from jax.experimental import pallas as pl
from jax.experimental.pallas import tpu as pltpu
from jax.sharding import PartitionSpec as P

HDIM = 128
MAX_TILES = 4
QBLK = 128


def layer_norm(row_data, norm_gain):
    values = row_data.astype(jnp.float32)
    center = values - jnp.mean(values, axis=1, keepdims=True)
    spread = jnp.mean(center * center, axis=1, keepdims=True)
    return (center * lax.rsqrt(spread + 1e-05) * norm_gain).astype(jnp.bfloat16)


def select_rows(row_data, wanted):
    flat = wanted.reshape(-1)
    hot = (flat[:, None] == jnp.arange(row_data.shape[0], dtype=jnp.int32)[None, :]).astype(jnp.bfloat16)
    picked = jnp.dot(hot, row_data, preferred_element_type=jnp.float32).astype(jnp.bfloat16)
    return picked.reshape(wanted.shape + (row_data.shape[1],))


def attend_kernel(mask_ref, q_ref, kv_ref, o_ref):
    tokens, width = q_ref.shape
    slots = kv_ref.shape[0]
    groups = kv_ref.shape[1] // (2 * HDIM)
    per_group = width // (groups * HDIM)
    tile_rows = slots // MAX_TILES
    scale = 1.0 / math.sqrt(HDIM)
    blocks = mask_ref.shape[0]
    slot = lax.broadcasted_iota(jnp.int32, (QBLK, slots), 1)
    for b in range(blocks):
        seen = jnp.zeros((QBLK, slots), jnp.float32)
        for tile in range(MAX_TILES):
            inside = (slot >= tile * tile_rows) & (slot < (tile + 1) * tile_rows)
            seen = jnp.where(inside, (mask_ref[b, tile] > 0).astype(jnp.float32), seen)
        visible = seen > 0.0
        rows = pl.ds(b * QBLK, QBLK)
        for g in range(groups):
            key_rows = kv_ref[:, g * 2 * HDIM:g * 2 * HDIM + HDIM]
            value_rows = kv_ref[:, g * 2 * HDIM + HDIM:(g + 1) * 2 * HDIM]
            for h in range(per_group):
                cols = pl.ds((g * per_group + h) * HDIM, HDIM)
                scores = lax.dot_general(
                    q_ref[rows, cols], key_rows, (((1,), (1,)), ((), ())),
                    preferred_element_type=jnp.float32) * scale
                masked = jnp.where(visible, scores, -1e30)
                top = jnp.max(masked, axis=1, keepdims=True)
                weights = jnp.where(visible, jnp.exp(masked - top), 0.0)
                total = jnp.sum(weights, axis=1, keepdims=True)
                total = jnp.where(total > 0.0, total, 1.0)
                probs = (weights / total).astype(jnp.bfloat16)
                o_ref[rows, cols] = jnp.dot(
                    probs, value_rows, preferred_element_type=jnp.float32).astype(jnp.bfloat16)


def attend(queries, kv_slots, block_mask):
    tokens, width = queries.shape
    return pl.pallas_call(
        attend_kernel,
        out_shape=jax.ShapeDtypeStruct((tokens, width), jnp.bfloat16),
        in_specs=[
            pl.BlockSpec(memory_space=pltpu.SMEM),
            pl.BlockSpec(memory_space=pltpu.VMEM),
            pl.BlockSpec(memory_space=pltpu.VMEM),
        ],
        out_specs=pl.BlockSpec(memory_space=pltpu.VMEM),
        cost_estimate=pl.CostEstimate(
            flops=4 * tokens * kv_slots.shape[0] * width, bytes_accessed=4 * tokens * width,
            transcendentals=tokens * kv_slots.shape[0] * width // HDIM),
        compiler_params=pltpu.CompilerParams(vmem_limit_bytes=24 * 1024 * 1024),
    )(block_mask, queries, kv_slots)


MESH = pl.DeviceIdType.MESH


def exchange_kernel(n_seq, n_tp, image_ref, gain_ref, want_ref, expand_any, shrink_any, proj_any, kvw_any,
                    states_ref, kv_ref,
                    expand_ref, shrink_ref, proj_ref, kvw_ref,
                    pair_out, pair_in, cross_out, cross_in, gathered, other, parts, parts_in, image_cut,
                    shares, chosen, slots,
                    l_s, a_s, a_r, c_s, c_r, b_s, b_r, g_r, up_s, down_s, y_s, x_s, m_r, v_s, v_r, s_s, s_r, f_s, f_r):
    s = lax.axis_index("seq")
    t = lax.axis_index("tp")
    z, y = s // 2, s % 2
    x, c = t // 2, t % 2
    last = n_tp - 1
    core, over, skew = 2 * x + 1 - c, 2 * (1 - x) + c, 2 * (1 - x) + 1 - c
    depth = proj_ref.shape[0] // n_tp
    half = 2 * depth
    cap = want_ref.shape[2]

    barrier = pltpu.get_barrier_semaphore()
    for j in range(1, n_tp):
        pl.semaphore_signal(barrier, inc=1, device_id=(s, lax.rem(t + j, n_tp)), device_id_type=MESH)
    for j in range(1, n_seq):
        pl.semaphore_signal(barrier, inc=1, device_id=(lax.rem(s + j, n_seq), t), device_id_type=MESH)

    def half_rows(h):
        return pl.ds(pl.multiple_of(h * half, 128), half)

    loads = [
        pltpu.make_async_copy(kvw_any, kvw_ref, l_s.at[0]),
        pltpu.make_async_copy(proj_any.at[half_rows(1 - c)], proj_ref.at[half_rows(1 - c)], l_s.at[1]),
        pltpu.make_async_copy(proj_any.at[half_rows(c)], proj_ref.at[half_rows(c)], l_s.at[2]),
        pltpu.make_async_copy(expand_any, expand_ref, l_s.at[3]),
        pltpu.make_async_copy(shrink_any, shrink_ref, l_s.at[4]),
    ]
    for load in loads:
        load.start()

    def remote(src, dst, send, recv, where):
        return pltpu.make_async_remote_copy(src_ref=src, dst_ref=dst, send_sem=send, recv_sem=recv,
                                            device_id=where, device_id_type=MESH)

    def arrive(buf, sem):
        pltpu.make_async_copy(buf, buf, sem).wait()

    sent = []

    def go(copy):
        copy.start()
        sent.append(copy)

    def fold_half(h):
        return jnp.dot(proj_ref[half_rows(h), :], kvw_ref[...], preferred_element_type=jnp.float32)

    loads[0].wait()
    loads[1].wait()
    pair_out[...] = fold_half(1 - c).astype(jnp.bfloat16)
    pl.semaphore_wait(barrier, n_tp + n_seq - 2)
    go(remote(pair_out, pair_in, a_s, a_r, (s, core)))
    loads[2].wait()
    own_fold = fold_half(c)
    arrive(pair_in, a_r)
    own_fold += pair_in[...].astype(jnp.float32)
    cross_out[...] = own_fold.astype(jnp.bfloat16)
    holds = z // 2 == x

    def cross():
        return remote(cross_out, cross_in, c_s, c_r, (s, over))

    @pl.when(z // 2 != x)
    def _():
        cross().start()

    values = image_ref[...].astype(jnp.float32)
    center = values - jnp.mean(values, axis=1, keepdims=True)
    spread = jnp.mean(center * center, axis=1, keepdims=True)
    normed = (center * lax.rsqrt(spread + 1e-05) * gain_ref[...][None, :]).astype(jnp.bfloat16)
    loads[3].wait()
    wide = jnp.dot(normed, expand_ref[...], preferred_element_type=jnp.float32)
    hidden = (0.5 * wide * (1.0 + lax.erf(wide * math.sqrt(0.5)))).astype(jnp.bfloat16)
    loads[4].wait()
    partial = jnp.dot(hidden, shrink_ref[...], preferred_element_type=jnp.float32)
    for q in range(n_tp):
        parts[q] = partial[:, q * depth:(q + 1) * depth].astype(jnp.bfloat16)
        image_cut[q] = values[:, q * depth:(q + 1) * depth]
    for j in range(1, n_tp):
        peer = lax.rem(t + j, n_tp)
        go(remote(parts.at[peer], parts_in.at[j], b_s.at[j], b_r.at[j], (s, peer)))

    def place(zl, yy, ch):
        return (zl * 2 + yy) * 2 + ch

    def up(i):
        return remote(gathered.at[i], gathered.at[i], up_s.at[i], g_r.at[i], (s + 2, t))

    def down(i):
        return remote(gathered.at[i], gathered.at[i], down_s.at[i], g_r.at[i], (s - 2, t))

    def across(i):
        return remote(gathered.at[i], gathered.at[i], y_s.at[i], g_r.at[i], (2 * z + 1 - y, t))

    def hand(i, k):
        return remote(gathered.at[i], other.at[k], x_s.at[i], m_r.at[k], (s, core))

    def hand_on(zl, yy, ch):
        @pl.when(zl != c)
        def _():
            hand(place(zl, yy, ch), 2 * yy + ch).start()

    def relay(zl, ch):
        i = place(zl, y, ch)
        zz = 2 * x + zl

        @pl.when(z != zz)
        def _():
            arrive(gathered.at[i], g_r.at[i])

        @pl.when((z >= zz) & (z < last))
        def _():
            up(i).start()

        @pl.when((z <= zz) & (z > 0))
        def _():
            down(i).start()

        across(i).start()
        hand_on(zl, y, ch)

    def y_relay(zl, ch):
        i = place(zl, 1 - y, ch)
        arrive(gathered.at[i], g_r.at[i])
        hand_on(zl, 1 - y, ch)

    first = (z + 2 * (1 - x)) // last
    second = 1 - first

    @pl.when(holds)
    def _():
        arrive(cross_in, c_r)
        for ch in range(2):
            rows = slice(ch * depth, (ch + 1) * depth)
            gathered[place(first, y, ch)] = (
                cross_out[rows, :].astype(jnp.float32) + cross_in[rows, :].astype(jnp.float32)).astype(jnp.bfloat16)
            relay(first, ch)

    share = parts[t].astype(jnp.float32)
    for j in range(1, n_tp):
        arrive(parts_in.at[j], b_r.at[j])
        share += parts_in[j].astype(jnp.float32)
    share = (image_cut[t] + share).astype(jnp.bfloat16)
    shares[t] = share
    row_id = lax.broadcasted_iota(jnp.int32, (share.shape[0], cap), 0)
    for d in range(n_seq):
        hot = (row_id == want_ref[0, d:d + 1, :]).astype(jnp.float32).astype(jnp.bfloat16)
        chosen[d] = lax.dot_general(
            hot, share, (((0,), (0,)), ((), ())), preferred_element_type=jnp.float32).astype(jnp.bfloat16)
    slots[t, s] = chosen[s]
    for j in range(1, n_seq):
        peer = lax.rem(s + j, n_seq)
        go(remote(chosen.at[peer], slots.at[t, s], s_s.at[j], s_r.at[s], (peer, t)))
    go(remote(shares.at[t], shares.at[t], v_s.at[1], v_r.at[t], (s, core)))
    go(remote(shares.at[t], shares.at[t], v_s.at[2], v_r.at[t], (s, over)))

    @pl.when(z // 2 != x)
    def _():
        for ch in range(2):
            relay(first, ch)

    for j in range(1, n_seq):
        peer = lax.rem(s + j, n_seq)
        arrive(slots.at[t, peer], s_r.at[peer])
    go(remote(slots.at[t], slots.at[t], f_s.at[1], f_r.at[t], (s, core)))
    go(remote(slots.at[t], slots.at[t], f_s.at[2], f_r.at[t], (s, over)))
    arrive(shares.at[over], v_r.at[over])
    go(remote(shares.at[over], shares.at[over], v_s.at[3], v_r.at[over], (s, core)))
    relay(second, 0)
    y_relay(first, 0)
    relay(second, 1)
    y_relay(first, 1)
    arrive(slots.at[over], f_r.at[over])
    go(remote(slots.at[over], slots.at[over], f_s.at[3], f_r.at[over], (s, core)))

    arrive(shares.at[core], v_r.at[core])
    arrive(shares.at[skew], v_r.at[skew])
    n_cut = 4
    cut = states_ref.shape[1] // n_cut
    for n in range(n_cut):
        cols = slice(n * cut, (n + 1) * cut)
        total = None
        for q in range(n_tp):
            term = jnp.dot(shares[q], proj_ref[q * depth:(q + 1) * depth, cols], preferred_element_type=jnp.float32)
            total = term if total is None else total + term
        states_ref[:, cols] = total.astype(jnp.bfloat16)

    arrive(slots.at[core], f_r.at[core])
    arrive(slots.at[skew], f_r.at[skew])
    for ch in range(2):
        y_relay(second, ch)
    width = kvw_ref.shape[1]
    for yy in range(2):
        total = None
        for ch in range(2):
            rows = slots[2 * c + ch].reshape(n_seq * cap, depth)
            term = jnp.dot(rows, gathered[place(c, yy, ch)], preferred_element_type=jnp.float32)
            total = term if total is None else total + term
        for ch in range(2):
            arrive(other.at[2 * yy + ch], m_r.at[2 * yy + ch])
            rows = slots[2 * (1 - c) + ch].reshape(n_seq * cap, depth)
            total += jnp.dot(rows, other[2 * yy + ch], preferred_element_type=jnp.float32)
        kv_ref[:, yy * width:(yy + 1) * width] = total.astype(jnp.bfloat16)

    for copy in sent:
        copy.wait_send()

    @pl.when(z // 2 != x)
    def _():
        cross().wait_send()

    for zl in range(2):
        zz = 2 * x + zl
        for ch in range(2):
            i = place(zl, y, ch)
            across(i).wait_send()

            @pl.when((z >= zz) & (z < last))
            def _():
                up(i).wait_send()

            @pl.when((z <= zz) & (z > 0))
            def _():
                down(i).wait_send()

            @pl.when(zl != c)
            def _():
                for yy in range(2):
                    hand(place(zl, yy, ch), 2 * yy + ch).wait_send()


def exchange(n_seq, n_tp, image_rows, norm_gain, send_list, expand_weight, shrink_weight, projector, kv_weight):
    rows, features = image_rows.shape
    depth = features // n_tp
    width = kv_weight.shape[1]
    cap = send_list.shape[2]
    bf16, f32 = jnp.bfloat16, jnp.float32
    dma = pltpu.SemaphoreType.DMA
    vmem = pl.BlockSpec(memory_space=pltpu.VMEM)
    anywhere = pl.BlockSpec(memory_space=pl.ANY)
    return pl.pallas_call(
        functools.partial(exchange_kernel, n_seq, n_tp),
        out_shape=(jax.ShapeDtypeStruct((rows, projector.shape[1]), bf16),
                   jax.ShapeDtypeStruct((n_seq * cap, 2 * width), bf16)),
        in_specs=[vmem] * 3 + [anywhere] * 4,
        out_specs=(vmem, vmem),
        scratch_shapes=[
            pltpu.VMEM(expand_weight.shape, bf16),
            pltpu.VMEM(shrink_weight.shape, bf16),
            pltpu.VMEM(projector.shape, bf16),
            pltpu.VMEM(kv_weight.shape, bf16),
            pltpu.VMEM((2 * depth, width), bf16),
            pltpu.VMEM((2 * depth, width), bf16),
            pltpu.VMEM((2 * depth, width), bf16),
            pltpu.VMEM((2 * depth, width), bf16),
            pltpu.VMEM((8, depth, width), bf16),
            pltpu.VMEM((4, depth, width), bf16),
            pltpu.VMEM((n_tp, rows, depth), bf16),
            pltpu.VMEM((n_tp, rows, depth), bf16),
            pltpu.VMEM((n_tp, rows, depth), f32),
            pltpu.VMEM((n_tp, rows, depth), bf16),
            pltpu.VMEM((n_seq, cap, depth), bf16),
            pltpu.VMEM((n_tp, n_seq, cap, depth), bf16),
            dma((5,)), dma, dma, dma, dma, dma((n_tp,)), dma((n_tp,)),
            dma((8,)), dma((8,)), dma((8,)), dma((8,)), dma((8,)), dma((4,)),
            dma((n_tp,)), dma((n_tp,)), dma((n_seq,)), dma((n_seq,)), dma((n_tp,)), dma((n_tp,)),
        ],
        compiler_params=pltpu.CompilerParams(
            collective_id=0, has_side_effects=True, vmem_limit_bytes=56 * 1024 * 1024),
    )(image_rows, norm_gain, send_list, expand_weight, shrink_weight, projector, kv_weight)


def local(
    image_rows,
    norm_gain,
    expand_weight,
    shrink_weight,
    projector,
    kv_weight,
    queries,
    send_list,
    block_mask,
):
    wanted = send_list[0]
    n_seq, n_tp = lax.axis_size("seq"), lax.axis_size("tp")
    if n_seq == 8 and n_tp == 4 and kv_weight.shape[1] == 2 * HDIM and wanted.shape[1] % 16 == 0:
        states, kv_slots = exchange(
            n_seq, n_tp, image_rows, norm_gain, send_list, expand_weight, shrink_weight, projector, kv_weight)
        return (states, attend(queries, kv_slots, block_mask))
    fold_part = jnp.dot(projector, kv_weight, preferred_element_type=jnp.float32).astype(jnp.bfloat16)
    fold_rows = lax.psum_scatter(fold_part, "tp", scatter_dimension=0, tiled=True)
    fold_rows = lax.all_gather(fold_rows, "seq", axis=1, tiled=True)
    normed = layer_norm(image_rows, norm_gain)
    hidden = jax.nn.gelu(
        jnp.dot(normed, expand_weight, preferred_element_type=jnp.float32), approximate=False
    ).astype(jnp.bfloat16)
    partial_value = jnp.dot(hidden, shrink_weight, preferred_element_type=jnp.float32).astype(jnp.bfloat16)
    own_sum = lax.psum_scatter(partial_value, "tp", scatter_dimension=1, tiled=True)
    share_width = own_sum.shape[1]
    own_rows = lax.dynamic_slice_in_dim(
        image_rows, lax.axis_index("tp") * share_width, share_width, 1
    )
    own_share = (own_rows.astype(jnp.float32) + own_sum.astype(jnp.float32)).astype(jnp.bfloat16)
    vit_out = lax.all_gather(own_share, "tp", axis=1, tiled=True)
    states = jnp.dot(vit_out, projector, preferred_element_type=jnp.float32).astype(jnp.bfloat16)
    outgoing = select_rows(own_share, wanted)
    arrived = lax.all_to_all(outgoing, "seq", split_axis=0, concat_axis=0, tiled=True)
    slot_rows = arrived.reshape(-1, share_width)
    kv_part = jnp.dot(slot_rows, fold_rows, preferred_element_type=jnp.float32).astype(jnp.bfloat16)
    kv_slots = lax.psum_scatter(kv_part, "tp", scatter_dimension=1, tiled=True)
    return (states, attend(queries, kv_slots, block_mask))


def solution(mesh):
    placed = (
        P("seq", None),
        P(),
        P(None, "tp"),
        P("tp", None),
        P(None, "tp"),
        P("tp", "seq"),
        P("seq", "tp"),
        P("seq", None, None),
        P("seq", None),
    )
    return jax.shard_map(
        local,
        mesh=mesh,
        in_specs=placed,
        out_specs=(P("seq", "tp"), P("seq", "tp")),
        check_vma=False,
    )
```

```python
import functools
import math

import jax
import jax.numpy as jnp
from jax import lax
from jax.experimental import pallas as pl
from jax.experimental.pallas import tpu as pltpu
from jax.sharding import PartitionSpec as P

HDIM = 128
MAX_TILES = 4
QBLK = 128


def layer_norm(row_data, norm_gain):
    values = row_data.astype(jnp.float32)
    center = values - jnp.mean(values, axis=1, keepdims=True)
    spread = jnp.mean(center * center, axis=1, keepdims=True)
    return (center * lax.rsqrt(spread + 1e-05) * norm_gain).astype(jnp.bfloat16)


def select_rows(row_data, wanted):
    flat = wanted.reshape(-1)
    hot = (flat[:, None] == jnp.arange(row_data.shape[0], dtype=jnp.int32)[None, :]).astype(jnp.bfloat16)
    picked = jnp.dot(hot, row_data, preferred_element_type=jnp.float32).astype(jnp.bfloat16)
    return picked.reshape(wanted.shape + (row_data.shape[1],))


def attend_kernel(moves, mask_ref, q_any, kv_ref, *refs):
    if moves:
        carried, o_ref, carried_out, q_ref, q_sem, carry_sem = refs
        carry = pltpu.make_async_copy(carried, carried_out, carry_sem)
    else:
        o_ref, q_ref, q_sem = refs
    tokens, width = q_ref.shape
    slots = kv_ref.shape[0]
    groups = kv_ref.shape[1] // (2 * HDIM)
    per_group = width // (groups * HDIM)
    tile_rows = slots // MAX_TILES
    scale = 1.0 / math.sqrt(HDIM)
    blocks = mask_ref.shape[0]
    n_cut = width // (2 * HDIM)
    loads = []
    for n in range(n_cut):
        cols = pl.ds(n * 2 * HDIM, 2 * HDIM)
        loads.append(pltpu.make_async_copy(q_any.at[:, cols], q_ref.at[:, cols], q_sem.at[n]))
        loads[-1].start()
    if moves:
        carry.start()
    slot = lax.broadcasted_iota(jnp.int32, (QBLK, slots), 1)
    sights = []
    for b in range(blocks):
        seen = jnp.zeros((QBLK, slots), jnp.float32)
        for tile in range(MAX_TILES):
            inside = (slot >= tile * tile_rows) & (slot < (tile + 1) * tile_rows)
            seen = jnp.where(inside, (mask_ref[b, tile] > 0).astype(jnp.float32), seen)
        sights.append(seen > 0.0)
    for h in range(groups * per_group):
        if h % 2 == 0:
            loads[h // 2].wait()
        g = h // per_group
        key_rows = kv_ref[:, g * 2 * HDIM:g * 2 * HDIM + HDIM]
        value_rows = kv_ref[:, g * 2 * HDIM + HDIM:(g + 1) * 2 * HDIM]
        cols = pl.ds(h * HDIM, HDIM)
        for b in range(blocks):
            rows = pl.ds(b * QBLK, QBLK)
            scores = lax.dot_general(
                q_ref[rows, cols], key_rows, (((1,), (1,)), ((), ())), preferred_element_type=jnp.float32)
            masked = jnp.where(sights[b], scores, -1e30)
            top = jnp.max(masked, axis=1, keepdims=True)
            weights = jnp.exp((masked - top) * scale)
            total = jnp.sum(weights, axis=1, keepdims=True)
            inverse = jnp.where(top > -1e29, 1.0 / total, 0.0)
            summed = jnp.dot(weights.astype(jnp.bfloat16), value_rows, preferred_element_type=jnp.float32)
            o_ref[rows, cols] = (summed * inverse).astype(jnp.bfloat16)
    if moves:
        carry.wait()


def attend(queries, kv_slots, block_mask, carried=None):
    tokens, width = queries.shape
    moves = carried is not None
    anywhere = pl.BlockSpec(memory_space=pl.ANY)
    vmem = pl.BlockSpec(memory_space=pltpu.VMEM)
    shapes = [jax.ShapeDtypeStruct((tokens, width), jnp.bfloat16)]
    operands = [block_mask, queries, kv_slots]
    scratch = [pltpu.VMEM((tokens, width), jnp.bfloat16), pltpu.SemaphoreType.DMA((width // (2 * HDIM),))]
    if moves:
        shapes.append(jax.ShapeDtypeStruct(carried.shape, carried.dtype))
        operands.append(carried)
        scratch.append(pltpu.SemaphoreType.DMA)
    return pl.pallas_call(
        functools.partial(attend_kernel, moves),
        out_shape=tuple(shapes),
        in_specs=[pl.BlockSpec(memory_space=pltpu.SMEM), anywhere, vmem] + [anywhere] * moves,
        out_specs=tuple([vmem] + [anywhere] * moves),
        scratch_shapes=scratch,
        cost_estimate=pl.CostEstimate(
            flops=4 * tokens * kv_slots.shape[0] * width, bytes_accessed=4 * tokens * width,
            transcendentals=tokens * kv_slots.shape[0] * width // HDIM),
        compiler_params=pltpu.CompilerParams(vmem_limit_bytes=60 * 1024 * 1024),
    )(*operands)


MESH = pl.DeviceIdType.MESH


def exchange_kernel(n_seq, n_tp, image_ref, gain_ref, want_ref, expand_any, shrink_any, proj_any, kvw_any,
                    states_ref, kv_ref,
                    expand_ref, shrink_ref, proj_ref, kvw_ref,
                    pair_out, pair_in, cross_out, cross_in, gathered, other, parts, parts_in, image_cut,
                    shares, chosen, slots,
                    l_s, a_s, a_r, c_s, c_r, b_s, b_r, g_r, up_s, down_s, y_s, x_s, m_r, v_s, v_r, s_s, s_r, f_s, f_r):
    s = lax.axis_index("seq")
    t = lax.axis_index("tp")
    z, y = s // 2, s % 2
    x, c = t // 2, t % 2
    last = n_tp - 1
    core, over, skew = 2 * x + 1 - c, 2 * (1 - x) + c, 2 * (1 - x) + 1 - c
    depth = proj_ref.shape[0] // n_tp
    half = 2 * depth
    cap = want_ref.shape[2]

    barrier = pltpu.get_barrier_semaphore()
    for j in range(1, n_tp):
        pl.semaphore_signal(barrier, inc=1, device_id=(s, lax.rem(t + j, n_tp)), device_id_type=MESH)
    for j in range(1, n_seq):
        pl.semaphore_signal(barrier, inc=1, device_id=(lax.rem(s + j, n_seq), t), device_id_type=MESH)

    def half_rows(h):
        return pl.ds(pl.multiple_of(h * half, 128), half)

    loads = [
        pltpu.make_async_copy(kvw_any, kvw_ref, l_s.at[0]),
        pltpu.make_async_copy(proj_any.at[half_rows(1 - c)], proj_ref.at[half_rows(1 - c)], l_s.at[1]),
        pltpu.make_async_copy(proj_any.at[half_rows(c)], proj_ref.at[half_rows(c)], l_s.at[2]),
        pltpu.make_async_copy(expand_any, expand_ref, l_s.at[3]),
        pltpu.make_async_copy(shrink_any, shrink_ref, l_s.at[4]),
    ]
    for load in loads:
        load.start()

    def remote(src, dst, send, recv, where):
        return pltpu.make_async_remote_copy(src_ref=src, dst_ref=dst, send_sem=send, recv_sem=recv,
                                            device_id=where, device_id_type=MESH)

    def arrive(buf, sem):
        pltpu.make_async_copy(buf, buf, sem).wait()

    sent = []

    def go(copy):
        copy.start()
        sent.append(copy)

    def fold_half(h):
        return jnp.dot(proj_ref[half_rows(h), :], kvw_ref[...], preferred_element_type=jnp.float32)

    loads[0].wait()
    loads[1].wait()
    pair_out[...] = fold_half(1 - c).astype(jnp.bfloat16)
    pl.semaphore_wait(barrier, n_tp + n_seq - 2)
    go(remote(pair_out, pair_in, a_s, a_r, (s, core)))
    loads[2].wait()
    own_fold = fold_half(c)
    arrive(pair_in, a_r)
    own_fold += pair_in[...].astype(jnp.float32)
    for ch in range(2):
        cross_out[ch] = own_fold[ch * depth:(ch + 1) * depth, :].astype(jnp.bfloat16)
    holds = z // 2 == x
    passes = z // 2 != x

    def cross(ch):
        return remote(cross_out.at[ch], cross_in.at[ch], c_s.at[ch], c_r.at[ch], (s, over))

    @pl.when(passes)
    def _():
        for ch in range(2):
            cross(ch).start()

    def place(zl, yy, ch):
        return (zl * 2 + yy) * 2 + ch

    def up(i):
        return remote(gathered.at[i], gathered.at[i], up_s.at[i], g_r.at[i], (s + 2, t))

    def down(i):
        return remote(gathered.at[i], gathered.at[i], down_s.at[i], g_r.at[i], (s - 2, t))

    def across(i):
        return remote(gathered.at[i], gathered.at[i], y_s.at[i], g_r.at[i], (2 * z + 1 - y, t))

    def hand(i, k):
        return remote(gathered.at[i], other.at[k], x_s.at[i], m_r.at[k], (s, core))

    def hand_on(zl, yy, ch):
        @pl.when(zl != c)
        def _():
            hand(place(zl, yy, ch), 2 * yy + ch).start()

    def relay(zl, ch):
        i = place(zl, y, ch)
        zz = 2 * x + zl

        @pl.when(z != zz)
        def _():
            arrive(gathered.at[i], g_r.at[i])

        @pl.when((z >= zz) & (z < last))
        def _():
            up(i).start()

        @pl.when((z <= zz) & (z > 0))
        def _():
            down(i).start()

        across(i).start()
        hand_on(zl, y, ch)

    def y_relay(zl, ch):
        i = place(zl, 1 - y, ch)
        arrive(gathered.at[i], g_r.at[i])
        hand_on(zl, 1 - y, ch)

    first = (z + 2 * (1 - x)) // last
    second = 1 - first

    def begin(ch):
        @pl.when(holds)
        def _():
            arrive(cross_in.at[ch], c_r.at[ch])
            gathered[place(first, y, ch)] = (
                cross_out[ch].astype(jnp.float32) + cross_in[ch].astype(jnp.float32)).astype(jnp.bfloat16)
            relay(first, ch)

    values = image_ref[...].astype(jnp.float32)
    center = values - jnp.mean(values, axis=1, keepdims=True)
    spread = jnp.mean(center * center, axis=1, keepdims=True)
    normed = (center * lax.rsqrt(spread + 1e-05) * gain_ref[...][None, :]).astype(jnp.bfloat16)
    loads[3].wait()
    wide = jnp.dot(normed, expand_ref[...], preferred_element_type=jnp.float32)
    hidden = (0.5 * wide * (1.0 + lax.erf(wide * math.sqrt(0.5)))).astype(jnp.bfloat16)
    begin(0)
    loads[4].wait()
    partial = jnp.dot(hidden, shrink_ref[...], preferred_element_type=jnp.float32)
    for q in range(n_tp):
        parts[q] = partial[:, q * depth:(q + 1) * depth].astype(jnp.bfloat16)
        image_cut[q] = values[:, q * depth:(q + 1) * depth]
    for j in range(1, n_tp):
        peer = lax.rem(t + j, n_tp)
        go(remote(parts.at[peer], parts_in.at[j], b_s.at[j], b_r.at[j], (s, peer)))

    begin(1)

    share = parts[t].astype(jnp.float32)
    for j in range(1, n_tp):
        arrive(parts_in.at[j], b_r.at[j])
        share += parts_in[j].astype(jnp.float32)
    share = (image_cut[t] + share).astype(jnp.bfloat16)
    shares[t] = share
    row_id = lax.broadcasted_iota(jnp.int32, (share.shape[0], cap), 0)
    for d in range(n_seq):
        hot = (row_id == want_ref[0, d:d + 1, :]).astype(jnp.float32).astype(jnp.bfloat16)
        chosen[d] = lax.dot_general(
            hot, share, (((0,), (0,)), ((), ())), preferred_element_type=jnp.float32).astype(jnp.bfloat16)
    slots[t, s] = chosen[s]
    for j in range(1, n_seq):
        peer = lax.rem(s + j, n_seq)
        go(remote(chosen.at[peer], slots.at[t, s], s_s.at[j], s_r.at[s], (peer, t)))
    go(remote(shares.at[t], shares.at[t], v_s.at[1], v_r.at[t], (s, core)))
    go(remote(shares.at[t], shares.at[t], v_s.at[2], v_r.at[t], (s, over)))

    @pl.when(passes)
    def _():
        for ch in range(2):
            relay(first, ch)

    @pl.when(holds)
    def _():
        for ch in range(2):
            relay(second, ch)

    for j in range(1, n_seq):
        peer = lax.rem(s + j, n_seq)
        arrive(slots.at[t, peer], s_r.at[peer])
    go(remote(slots.at[t], slots.at[t], f_s.at[1], f_r.at[t], (s, core)))
    go(remote(slots.at[t], slots.at[t], f_s.at[2], f_r.at[t], (s, over)))
    arrive(shares.at[over], v_r.at[over])
    go(remote(shares.at[over], shares.at[over], v_s.at[3], v_r.at[over], (s, core)))
    for ch in range(2):
        @pl.when(passes)
        def _():
            relay(second, ch)
        y_relay(first, ch)
    arrive(slots.at[over], f_r.at[over])
    go(remote(slots.at[over], slots.at[over], f_s.at[3], f_r.at[over], (s, core)))

    arrive(shares.at[core], v_r.at[core])
    arrive(shares.at[skew], v_r.at[skew])
    n_cut = 4
    cut = states_ref.shape[1] // n_cut
    for n in range(n_cut):
        cols = slice(n * cut, (n + 1) * cut)
        total = None
        for q in range(n_tp):
            term = jnp.dot(shares[q], proj_ref[q * depth:(q + 1) * depth, cols], preferred_element_type=jnp.float32)
            total = term if total is None else total + term
        states_ref[:, cols] = total.astype(jnp.bfloat16)

    arrive(slots.at[core], f_r.at[core])
    arrive(slots.at[skew], f_r.at[skew])
    for ch in range(2):
        y_relay(second, ch)
    width = kvw_ref.shape[1]
    for yy in range(2):
        total = None
        for ch in range(2):
            rows = slots[2 * c + ch].reshape(n_seq * cap, depth)
            term = jnp.dot(rows, gathered[place(c, yy, ch)], preferred_element_type=jnp.float32)
            total = term if total is None else total + term
        for ch in range(2):
            arrive(other.at[2 * yy + ch], m_r.at[2 * yy + ch])
            rows = slots[2 * (1 - c) + ch].reshape(n_seq * cap, depth)
            total += jnp.dot(rows, other[2 * yy + ch], preferred_element_type=jnp.float32)
        kv_ref[:, yy * width:(yy + 1) * width] = total.astype(jnp.bfloat16)

    for copy in sent:
        copy.wait_send()

    @pl.when(passes)
    def _():
        for ch in range(2):
            cross(ch).wait_send()

    for zl in range(2):
        zz = 2 * x + zl
        for ch in range(2):
            i = place(zl, y, ch)
            across(i).wait_send()

            @pl.when((z >= zz) & (z < last))
            def _():
                up(i).wait_send()

            @pl.when((z <= zz) & (z > 0))
            def _():
                down(i).wait_send()

            @pl.when(zl != c)
            def _():
                for yy in range(2):
                    hand(place(zl, yy, ch), 2 * yy + ch).wait_send()


def exchange(n_seq, n_tp, image_rows, norm_gain, send_list, expand_weight, shrink_weight, projector, kv_weight):
    rows, features = image_rows.shape
    depth = features // n_tp
    width = kv_weight.shape[1]
    cap = send_list.shape[2]
    bf16, f32 = jnp.bfloat16, jnp.float32
    dma = pltpu.SemaphoreType.DMA
    vmem = pl.BlockSpec(memory_space=pltpu.VMEM)
    anywhere = pl.BlockSpec(memory_space=pl.ANY)
    return pl.pallas_call(
        functools.partial(exchange_kernel, n_seq, n_tp),
        out_shape=(jax.ShapeDtypeStruct((rows, projector.shape[1]), bf16),
                   jax.ShapeDtypeStruct((n_seq * cap, 2 * width), bf16)),
        in_specs=[vmem] * 3 + [anywhere] * 4,
        out_specs=(vmem, vmem),
        scratch_shapes=[
            pltpu.VMEM(expand_weight.shape, bf16),
            pltpu.VMEM(shrink_weight.shape, bf16),
            pltpu.VMEM(projector.shape, bf16),
            pltpu.VMEM(kv_weight.shape, bf16),
            pltpu.VMEM((2 * depth, width), bf16),
            pltpu.VMEM((2 * depth, width), bf16),
            pltpu.VMEM((2, depth, width), bf16),
            pltpu.VMEM((2, depth, width), bf16),
            pltpu.VMEM((8, depth, width), bf16),
            pltpu.VMEM((4, depth, width), bf16),
            pltpu.VMEM((n_tp, rows, depth), bf16),
            pltpu.VMEM((n_tp, rows, depth), bf16),
            pltpu.VMEM((n_tp, rows, depth), f32),
            pltpu.VMEM((n_tp, rows, depth), bf16),
            pltpu.VMEM((n_seq, cap, depth), bf16),
            pltpu.VMEM((n_tp, n_seq, cap, depth), bf16),
            dma((5,)), dma, dma, dma((2,)), dma((2,)), dma((n_tp,)), dma((n_tp,)),
            dma((8,)), dma((8,)), dma((8,)), dma((8,)), dma((8,)), dma((4,)),
            dma((n_tp,)), dma((n_tp,)), dma((n_seq,)), dma((n_seq,)), dma((n_tp,)), dma((n_tp,)),
        ],
        compiler_params=pltpu.CompilerParams(
            collective_id=0, has_side_effects=True, vmem_limit_bytes=56 * 1024 * 1024),
    )(image_rows, norm_gain, send_list, expand_weight, shrink_weight, projector, kv_weight)


def local(
    image_rows,
    norm_gain,
    expand_weight,
    shrink_weight,
    projector,
    kv_weight,
    queries,
    send_list,
    block_mask,
):
    wanted = send_list[0]
    n_seq, n_tp = lax.axis_size("seq"), lax.axis_size("tp")
    if n_seq == 8 and n_tp == 4 and kv_weight.shape[1] == 2 * HDIM and wanted.shape[1] % 16 == 0:
        states, kv_slots = exchange(
            n_seq, n_tp, image_rows, norm_gain, send_list, expand_weight, shrink_weight, projector, kv_weight)
        context, states = attend(queries, kv_slots, block_mask, states)
        return (states, context)
    fold_part = jnp.dot(projector, kv_weight, preferred_element_type=jnp.float32).astype(jnp.bfloat16)
    fold_rows = lax.psum_scatter(fold_part, "tp", scatter_dimension=0, tiled=True)
    fold_rows = lax.all_gather(fold_rows, "seq", axis=1, tiled=True)
    normed = layer_norm(image_rows, norm_gain)
    hidden = jax.nn.gelu(
        jnp.dot(normed, expand_weight, preferred_element_type=jnp.float32), approximate=False
    ).astype(jnp.bfloat16)
    partial_value = jnp.dot(hidden, shrink_weight, preferred_element_type=jnp.float32).astype(jnp.bfloat16)
    own_sum = lax.psum_scatter(partial_value, "tp", scatter_dimension=1, tiled=True)
    share_width = own_sum.shape[1]
    own_rows = lax.dynamic_slice_in_dim(
        image_rows, lax.axis_index("tp") * share_width, share_width, 1
    )
    own_share = (own_rows.astype(jnp.float32) + own_sum.astype(jnp.float32)).astype(jnp.bfloat16)
    vit_out = lax.all_gather(own_share, "tp", axis=1, tiled=True)
    states = jnp.dot(vit_out, projector, preferred_element_type=jnp.float32).astype(jnp.bfloat16)
    outgoing = select_rows(own_share, wanted)
    arrived = lax.all_to_all(outgoing, "seq", split_axis=0, concat_axis=0, tiled=True)
    slot_rows = arrived.reshape(-1, share_width)
    kv_part = jnp.dot(slot_rows, fold_rows, preferred_element_type=jnp.float32).astype(jnp.bfloat16)
    kv_slots = lax.psum_scatter(kv_part, "tp", scatter_dimension=1, tiled=True)
    return (states, attend(queries, kv_slots, block_mask)[0])


def solution(mesh):
    placed = (
        P("seq", None),
        P(),
        P(None, "tp"),
        P("tp", None),
        P(None, "tp"),
        P("tp", "seq"),
        P("seq", "tp"),
        P("seq", None, None),
        P("seq", None),
    )
    return jax.shard_map(
        local,
        mesh=mesh,
        in_specs=placed,
        out_specs=(P("seq", "tp"), P("seq", "tp")),
        check_vma=False,
    )
```

```python
import functools
import math

import jax
import jax.numpy as jnp
from jax import lax
from jax.experimental import pallas as pl
from jax.experimental.pallas import tpu as pltpu
from jax.sharding import PartitionSpec as P

HDIM = 128
MAX_TILES = 4
QBLK = 128


def layer_norm(row_data, norm_gain):
    values = row_data.astype(jnp.float32)
    center = values - jnp.mean(values, axis=1, keepdims=True)
    spread = jnp.mean(center * center, axis=1, keepdims=True)
    return (center * lax.rsqrt(spread + 1e-05) * norm_gain).astype(jnp.bfloat16)


def select_rows(row_data, wanted):
    flat = wanted.reshape(-1)
    hot = (flat[:, None] == jnp.arange(row_data.shape[0], dtype=jnp.int32)[None, :]).astype(jnp.bfloat16)
    picked = jnp.dot(hot, row_data, preferred_element_type=jnp.float32).astype(jnp.bfloat16)
    return picked.reshape(wanted.shape + (row_data.shape[1],))


def attend_kernel(moves, mask_ref, q_ref, kv_ref, *refs):
    if moves:
        carried, o_ref, carried_out, held, carry_sem = refs
        carry_in = pltpu.make_async_copy(carried, held, carry_sem.at[0])
        carry_out = pltpu.make_async_copy(held, carried_out, carry_sem.at[1])
        carry_in.start()
    else:
        o_ref, = refs
    tokens, width = q_ref.shape
    slots = kv_ref.shape[0]
    groups = kv_ref.shape[1] // (2 * HDIM)
    per_group = width // (groups * HDIM)
    tile_rows = slots // MAX_TILES
    scale = 1.0 / math.sqrt(HDIM)
    blocks = mask_ref.shape[0]
    slot = lax.broadcasted_iota(jnp.int32, (QBLK, slots), 1)
    sights = []
    for b in range(blocks):
        seen = jnp.zeros((QBLK, slots), jnp.float32)
        for tile in range(MAX_TILES):
            inside = (slot >= tile * tile_rows) & (slot < (tile + 1) * tile_rows)
            seen = jnp.where(inside, (mask_ref[b, tile] > 0).astype(jnp.float32), seen)
        sights.append(seen > 0.0)
    for h in range(groups * per_group):
        if moves and h == groups * per_group // 2:
            carry_in.wait()
            carry_out.start()
        g = h // per_group
        key_rows = kv_ref[:, g * 2 * HDIM:g * 2 * HDIM + HDIM]
        value_rows = kv_ref[:, g * 2 * HDIM + HDIM:(g + 1) * 2 * HDIM]
        cols = pl.ds(h * HDIM, HDIM)
        for b in range(blocks):
            rows = pl.ds(b * QBLK, QBLK)
            scores = lax.dot_general(
                q_ref[rows, cols], key_rows, (((1,), (1,)), ((), ())), preferred_element_type=jnp.float32)
            masked = jnp.where(sights[b], scores, -1e30)
            top = jnp.max(masked, axis=1, keepdims=True)
            weights = jnp.exp((masked - top) * scale)
            total = jnp.sum(weights, axis=1, keepdims=True)
            inverse = jnp.where(top > -1e29, 1.0 / total, 0.0)
            summed = jnp.dot(weights.astype(jnp.bfloat16), value_rows, preferred_element_type=jnp.float32)
            o_ref[rows, cols] = (summed * inverse).astype(jnp.bfloat16)
    if moves:
        carry_out.wait()


def attend(queries, kv_slots, block_mask, carried=None):
    tokens, width = queries.shape
    moves = carried is not None
    anywhere = pl.BlockSpec(memory_space=pl.ANY)
    vmem = pl.BlockSpec(memory_space=pltpu.VMEM)
    shapes = [jax.ShapeDtypeStruct((tokens, width), jnp.bfloat16)]
    operands = [block_mask, queries, kv_slots]
    scratch = []
    if moves:
        shapes.append(jax.ShapeDtypeStruct(carried.shape, carried.dtype))
        operands.append(carried)
        scratch += [pltpu.VMEM(carried.shape, carried.dtype), pltpu.SemaphoreType.DMA((2,))]
    return pl.pallas_call(
        functools.partial(attend_kernel, moves),
        out_shape=tuple(shapes),
        in_specs=[pl.BlockSpec(memory_space=pltpu.SMEM), vmem, vmem] + [anywhere] * moves,
        out_specs=tuple([vmem] + [anywhere] * moves),
        scratch_shapes=scratch,
        cost_estimate=pl.CostEstimate(
            flops=4 * tokens * kv_slots.shape[0] * width, bytes_accessed=4 * tokens * width,
            transcendentals=tokens * kv_slots.shape[0] * width // HDIM),
        compiler_params=pltpu.CompilerParams(vmem_limit_bytes=60 * 1024 * 1024),
    )(*operands)


MESH = pl.DeviceIdType.MESH


def exchange_kernel(n_seq, n_tp, image_ref, gain_ref, want_ref, expand_any, shrink_any, proj_any, kvw_any,
                    states_ref, kv_ref,
                    expand_ref, shrink_ref, proj_ref, kvw_ref,
                    pair_out, pair_in, cross_out, cross_in, gathered, other, parts, parts_in, image_cut,
                    shares, chosen, slots,
                    l_s, a_s, a_r, c_s, c_r, b_s, b_r, g_r, up_s, down_s, y_s, x_s, m_r, v_s, v_r, s_s, s_r, f_s, f_r):
    s = lax.axis_index("seq")
    t = lax.axis_index("tp")
    z, y = s // 2, s % 2
    x, c = t // 2, t % 2
    last = n_tp - 1
    core, over, skew = 2 * x + 1 - c, 2 * (1 - x) + c, 2 * (1 - x) + 1 - c
    depth = proj_ref.shape[0] // n_tp
    half = 2 * depth
    cap = want_ref.shape[2]

    barrier = pltpu.get_barrier_semaphore()
    for j in range(1, n_tp):
        pl.semaphore_signal(barrier, inc=1, device_id=(s, lax.rem(t + j, n_tp)), device_id_type=MESH)
    for j in range(1, n_seq):
        pl.semaphore_signal(barrier, inc=1, device_id=(lax.rem(s + j, n_seq), t), device_id_type=MESH)

    def half_rows(h):
        return pl.ds(pl.multiple_of(h * half, 128), half)

    loads = [
        pltpu.make_async_copy(kvw_any, kvw_ref, l_s.at[0]),
        pltpu.make_async_copy(proj_any.at[half_rows(1 - c)], proj_ref.at[half_rows(1 - c)], l_s.at[1]),
        pltpu.make_async_copy(proj_any.at[half_rows(c)], proj_ref.at[half_rows(c)], l_s.at[2]),
        pltpu.make_async_copy(expand_any, expand_ref, l_s.at[3]),
        pltpu.make_async_copy(shrink_any, shrink_ref, l_s.at[4]),
    ]
    for load in loads:
        load.start()

    def remote(src, dst, send, recv, where):
        return pltpu.make_async_remote_copy(src_ref=src, dst_ref=dst, send_sem=send, recv_sem=recv,
                                            device_id=where, device_id_type=MESH)

    def arrive(buf, sem):
        pltpu.make_async_copy(buf, buf, sem).wait()

    sent = []

    def go(copy):
        copy.start()
        sent.append(copy)

    def fold_half(h):
        return jnp.dot(proj_ref[half_rows(h), :], kvw_ref[...], preferred_element_type=jnp.float32)

    loads[0].wait()
    loads[1].wait()
    pair_out[...] = fold_half(1 - c).astype(jnp.bfloat16)
    pl.semaphore_wait(barrier, n_tp + n_seq - 2)
    go(remote(pair_out, pair_in, a_s, a_r, (s, core)))
    loads[2].wait()
    own_fold = fold_half(c)
    arrive(pair_in, a_r)
    own_fold += pair_in[...].astype(jnp.float32)
    for ch in range(2):
        cross_out[ch] = own_fold[ch * depth:(ch + 1) * depth, :].astype(jnp.bfloat16)
    holds = z // 2 == x
    passes = z // 2 != x

    def cross(ch):
        return remote(cross_out.at[ch], cross_in.at[ch], c_s.at[ch], c_r.at[ch], (s, over))

    @pl.when(passes)
    def _():
        for ch in range(2):
            cross(ch).start()

    def place(zl, yy, ch):
        return (zl * 2 + yy) * 2 + ch

    def up(i):
        return remote(gathered.at[i], gathered.at[i], up_s.at[i], g_r.at[i], (s + 2, t))

    def down(i):
        return remote(gathered.at[i], gathered.at[i], down_s.at[i], g_r.at[i], (s - 2, t))

    def across(i):
        return remote(gathered.at[i], gathered.at[i], y_s.at[i], g_r.at[i], (2 * z + 1 - y, t))

    def hand(i, k):
        return remote(gathered.at[i], other.at[k], x_s.at[i], m_r.at[k], (s, core))

    def hand_on(zl, yy, ch):
        @pl.when(zl != c)
        def _():
            hand(place(zl, yy, ch), 2 * yy + ch).start()

    def relay(zl, ch):
        i = place(zl, y, ch)
        zz = 2 * x + zl

        @pl.when(z != zz)
        def _():
            arrive(gathered.at[i], g_r.at[i])

        @pl.when((z >= zz) & (z < last))
        def _():
            up(i).start()

        @pl.when((z <= zz) & (z > 0))
        def _():
            down(i).start()

        across(i).start()
        hand_on(zl, y, ch)

    def y_relay(zl, ch):
        i = place(zl, 1 - y, ch)
        arrive(gathered.at[i], g_r.at[i])
        hand_on(zl, 1 - y, ch)

    first = (z + 2 * (1 - x)) // last
    second = 1 - first

    def begin(ch):
        @pl.when(holds)
        def _():
            arrive(cross_in.at[ch], c_r.at[ch])
            gathered[place(first, y, ch)] = (
                cross_out[ch].astype(jnp.float32) + cross_in[ch].astype(jnp.float32)).astype(jnp.bfloat16)
            relay(first, ch)

    values = image_ref[...].astype(jnp.float32)
    center = values - jnp.mean(values, axis=1, keepdims=True)
    spread = jnp.mean(center * center, axis=1, keepdims=True)
    normed = (center * lax.rsqrt(spread + 1e-05) * gain_ref[...][None, :]).astype(jnp.bfloat16)
    loads[3].wait()
    wide = jnp.dot(normed, expand_ref[...], preferred_element_type=jnp.float32)
    hidden = (0.5 * wide * (1.0 + lax.erf(wide * math.sqrt(0.5)))).astype(jnp.bfloat16)
    begin(0)
    loads[4].wait()
    partial = jnp.dot(hidden, shrink_ref[...], preferred_element_type=jnp.float32)
    for q in range(n_tp):
        parts[q] = partial[:, q * depth:(q + 1) * depth].astype(jnp.bfloat16)
        image_cut[q] = values[:, q * depth:(q + 1) * depth]
    for j in range(1, n_tp):
        peer = lax.rem(t + j, n_tp)
        go(remote(parts.at[peer], parts_in.at[j], b_s.at[j], b_r.at[j], (s, peer)))

    begin(1)

    share = parts[t].astype(jnp.float32)
    for j in range(1, n_tp):
        arrive(parts_in.at[j], b_r.at[j])
        share += parts_in[j].astype(jnp.float32)
    share = (image_cut[t] + share).astype(jnp.bfloat16)
    shares[t] = share
    row_id = lax.broadcasted_iota(jnp.int32, (share.shape[0], cap), 0)
    for d in range(n_seq):
        hot = (row_id == want_ref[0, d:d + 1, :]).astype(jnp.float32).astype(jnp.bfloat16)
        chosen[d] = lax.dot_general(
            hot, share, (((0,), (0,)), ((), ())), preferred_element_type=jnp.float32).astype(jnp.bfloat16)
    slots[t, s] = chosen[s]
    for j in range(1, n_seq):
        peer = lax.rem(s + j, n_seq)
        go(remote(chosen.at[peer], slots.at[t, s], s_s.at[j], s_r.at[s], (peer, t)))
    go(remote(shares.at[t], shares.at[t], v_s.at[1], v_r.at[t], (s, core)))
    go(remote(shares.at[t], shares.at[t], v_s.at[2], v_r.at[t], (s, over)))

    @pl.when(passes)
    def _():
        for ch in range(2):
            relay(first, ch)

    @pl.when(holds)
    def _():
        for ch in range(2):
            relay(second, ch)

    for j in range(1, n_seq):
        peer = lax.rem(s + j, n_seq)
        arrive(slots.at[t, peer], s_r.at[peer])
    go(remote(slots.at[t], slots.at[t], f_s.at[1], f_r.at[t], (s, core)))
    go(remote(slots.at[t], slots.at[t], f_s.at[2], f_r.at[t], (s, over)))
    arrive(shares.at[over], v_r.at[over])
    go(remote(shares.at[over], shares.at[over], v_s.at[3], v_r.at[over], (s, core)))
    for ch in range(2):
        @pl.when(passes)
        def _():
            relay(second, ch)
        y_relay(first, ch)
    arrive(slots.at[over], f_r.at[over])
    go(remote(slots.at[over], slots.at[over], f_s.at[3], f_r.at[over], (s, core)))

    arrive(shares.at[core], v_r.at[core])
    arrive(shares.at[skew], v_r.at[skew])
    n_cut = 4
    cut = states_ref.shape[1] // n_cut
    for n in range(n_cut):
        cols = slice(n * cut, (n + 1) * cut)
        total = None
        for q in range(n_tp):
            term = jnp.dot(shares[q], proj_ref[q * depth:(q + 1) * depth, cols], preferred_element_type=jnp.float32)
            total = term if total is None else total + term
        states_ref[:, cols] = total.astype(jnp.bfloat16)

    arrive(slots.at[core], f_r.at[core])
    arrive(slots.at[skew], f_r.at[skew])
    for ch in range(2):
        y_relay(second, ch)
    width = kvw_ref.shape[1]
    for yy in range(2):
        total = None
        for ch in range(2):
            rows = slots[2 * c + ch].reshape(n_seq * cap, depth)
            term = jnp.dot(rows, gathered[place(c, yy, ch)], preferred_element_type=jnp.float32)
            total = term if total is None else total + term
        for ch in range(2):
            arrive(other.at[2 * yy + ch], m_r.at[2 * yy + ch])
            rows = slots[2 * (1 - c) + ch].reshape(n_seq * cap, depth)
            total += jnp.dot(rows, other[2 * yy + ch], preferred_element_type=jnp.float32)
        kv_ref[:, yy * width:(yy + 1) * width] = total.astype(jnp.bfloat16)

    for copy in sent:
        copy.wait_send()

    @pl.when(passes)
    def _():
        for ch in range(2):
            cross(ch).wait_send()

    for zl in range(2):
        zz = 2 * x + zl
        for ch in range(2):
            i = place(zl, y, ch)
            across(i).wait_send()

            @pl.when((z >= zz) & (z < last))
            def _():
                up(i).wait_send()

            @pl.when((z <= zz) & (z > 0))
            def _():
                down(i).wait_send()

            @pl.when(zl != c)
            def _():
                for yy in range(2):
                    hand(place(zl, yy, ch), 2 * yy + ch).wait_send()


def exchange(n_seq, n_tp, image_rows, norm_gain, send_list, expand_weight, shrink_weight, projector, kv_weight):
    rows, features = image_rows.shape
    depth = features // n_tp
    width = kv_weight.shape[1]
    cap = send_list.shape[2]
    bf16, f32 = jnp.bfloat16, jnp.float32
    dma = pltpu.SemaphoreType.DMA
    vmem = pl.BlockSpec(memory_space=pltpu.VMEM)
    anywhere = pl.BlockSpec(memory_space=pl.ANY)
    return pl.pallas_call(
        functools.partial(exchange_kernel, n_seq, n_tp),
        out_shape=(jax.ShapeDtypeStruct((rows, projector.shape[1]), bf16),
                   jax.ShapeDtypeStruct((n_seq * cap, 2 * width), bf16)),
        in_specs=[vmem] * 3 + [anywhere] * 4,
        out_specs=(vmem, vmem),
        scratch_shapes=[
            pltpu.VMEM(expand_weight.shape, bf16),
            pltpu.VMEM(shrink_weight.shape, bf16),
            pltpu.VMEM(projector.shape, bf16),
            pltpu.VMEM(kv_weight.shape, bf16),
            pltpu.VMEM((2 * depth, width), bf16),
            pltpu.VMEM((2 * depth, width), bf16),
            pltpu.VMEM((2, depth, width), bf16),
            pltpu.VMEM((2, depth, width), bf16),
            pltpu.VMEM((8, depth, width), bf16),
            pltpu.VMEM((4, depth, width), bf16),
            pltpu.VMEM((n_tp, rows, depth), bf16),
            pltpu.VMEM((n_tp, rows, depth), bf16),
            pltpu.VMEM((n_tp, rows, depth), f32),
            pltpu.VMEM((n_tp, rows, depth), bf16),
            pltpu.VMEM((n_seq, cap, depth), bf16),
            pltpu.VMEM((n_tp, n_seq, cap, depth), bf16),
            dma((5,)), dma, dma, dma((2,)), dma((2,)), dma((n_tp,)), dma((n_tp,)),
            dma((8,)), dma((8,)), dma((8,)), dma((8,)), dma((8,)), dma((4,)),
            dma((n_tp,)), dma((n_tp,)), dma((n_seq,)), dma((n_seq,)), dma((n_tp,)), dma((n_tp,)),
        ],
        compiler_params=pltpu.CompilerParams(
            collective_id=0, has_side_effects=True, vmem_limit_bytes=56 * 1024 * 1024),
    )(image_rows, norm_gain, send_list, expand_weight, shrink_weight, projector, kv_weight)


def local(
    image_rows,
    norm_gain,
    expand_weight,
    shrink_weight,
    projector,
    kv_weight,
    queries,
    send_list,
    block_mask,
):
    wanted = send_list[0]
    n_seq, n_tp = lax.axis_size("seq"), lax.axis_size("tp")
    if n_seq == 8 and n_tp == 4 and kv_weight.shape[1] == 2 * HDIM and wanted.shape[1] % 16 == 0:
        states, kv_slots = exchange(
            n_seq, n_tp, image_rows, norm_gain, send_list, expand_weight, shrink_weight, projector, kv_weight)
        context, states = attend(queries, kv_slots, block_mask, states)
        return (states, context)
    fold_part = jnp.dot(projector, kv_weight, preferred_element_type=jnp.float32).astype(jnp.bfloat16)
    fold_rows = lax.psum_scatter(fold_part, "tp", scatter_dimension=0, tiled=True)
    fold_rows = lax.all_gather(fold_rows, "seq", axis=1, tiled=True)
    normed = layer_norm(image_rows, norm_gain)
    hidden = jax.nn.gelu(
        jnp.dot(normed, expand_weight, preferred_element_type=jnp.float32), approximate=False
    ).astype(jnp.bfloat16)
    partial_value = jnp.dot(hidden, shrink_weight, preferred_element_type=jnp.float32).astype(jnp.bfloat16)
    own_sum = lax.psum_scatter(partial_value, "tp", scatter_dimension=1, tiled=True)
    share_width = own_sum.shape[1]
    own_rows = lax.dynamic_slice_in_dim(
        image_rows, lax.axis_index("tp") * share_width, share_width, 1
    )
    own_share = (own_rows.astype(jnp.float32) + own_sum.astype(jnp.float32)).astype(jnp.bfloat16)
    vit_out = lax.all_gather(own_share, "tp", axis=1, tiled=True)
    states = jnp.dot(vit_out, projector, preferred_element_type=jnp.float32).astype(jnp.bfloat16)
    outgoing = select_rows(own_share, wanted)
    arrived = lax.all_to_all(outgoing, "seq", split_axis=0, concat_axis=0, tiled=True)
    slot_rows = arrived.reshape(-1, share_width)
    kv_part = jnp.dot(slot_rows, fold_rows, preferred_element_type=jnp.float32).astype(jnp.bfloat16)
    kv_slots = lax.psum_scatter(kv_part, "tp", scatter_dimension=1, tiled=True)
    return (states, attend(queries, kv_slots, block_mask)[0])


def solution(mesh):
    placed = (
        P("seq", None),
        P(),
        P(None, "tp"),
        P("tp", None),
        P(None, "tp"),
        P("tp", "seq"),
        P("seq", "tp"),
        P("seq", None, None),
        P("seq", None),
    )
    return jax.shard_map(
        local,
        mesh=mesh,
        in_specs=placed,
        out_specs=(P("seq", "tp"), P("seq", "tp")),
        check_vma=False,
    )
```

```python
import functools
import math

import jax
import jax.numpy as jnp
from jax import lax
from jax.experimental import pallas as pl
from jax.experimental.pallas import tpu as pltpu
from jax.sharding import PartitionSpec as P

HDIM = 128
MAX_TILES = 4
QBLK = 128


def layer_norm(row_data, norm_gain):
    values = row_data.astype(jnp.float32)
    center = values - jnp.mean(values, axis=1, keepdims=True)
    spread = jnp.mean(center * center, axis=1, keepdims=True)
    return (center * lax.rsqrt(spread + 1e-05) * norm_gain).astype(jnp.bfloat16)


def select_rows(row_data, wanted):
    flat = wanted.reshape(-1)
    hot = (flat[:, None] == jnp.arange(row_data.shape[0], dtype=jnp.int32)[None, :]).astype(jnp.bfloat16)
    picked = jnp.dot(hot, row_data, preferred_element_type=jnp.float32).astype(jnp.bfloat16)
    return picked.reshape(wanted.shape + (row_data.shape[1],))


def attend_kernel(moves, mask_ref, q_ref, kv_ref, *refs):
    if moves:
        carried, o_ref, carried_out, held, carry_sem = refs
        carry_in = pltpu.make_async_copy(carried, held, carry_sem.at[0])
        carry_out = pltpu.make_async_copy(held, carried_out, carry_sem.at[1])
        carry_in.start()
    else:
        o_ref, = refs
    tokens, width = q_ref.shape
    slots = kv_ref.shape[0]
    groups = kv_ref.shape[1] // (2 * HDIM)
    per_group = width // (groups * HDIM)
    tile_rows = slots // MAX_TILES
    scale = 1.0 / math.sqrt(HDIM)
    blocks = mask_ref.shape[0]
    slot = lax.broadcasted_iota(jnp.int32, (QBLK, slots), 1)
    sights = []
    for b in range(blocks):
        seen = jnp.zeros((QBLK, slots), jnp.float32)
        for tile in range(MAX_TILES):
            inside = (slot >= tile * tile_rows) & (slot < (tile + 1) * tile_rows)
            seen = jnp.where(inside, (mask_ref[b, tile] > 0).astype(jnp.float32), seen)
        sights.append(seen > 0.0)
    for h in range(groups * per_group):
        if moves and h == groups * per_group // 2:
            carry_in.wait()
            carry_out.start()
        g = h // per_group
        key_rows = kv_ref[:, g * 2 * HDIM:g * 2 * HDIM + HDIM]
        value_rows = kv_ref[:, g * 2 * HDIM + HDIM:(g + 1) * 2 * HDIM]
        cols = pl.ds(h * HDIM, HDIM)
        for b in range(blocks):
            rows = pl.ds(b * QBLK, QBLK)
            scores = lax.dot_general(
                q_ref[rows, cols], key_rows, (((1,), (1,)), ((), ())), preferred_element_type=jnp.float32)
            masked = jnp.where(sights[b], scores, -1e30)
            top = jnp.max(masked, axis=1, keepdims=True)
            weights = jnp.exp((masked - top) * scale)
            total = jnp.sum(weights, axis=1, keepdims=True)
            inverse = jnp.where(top > -1e29, 1.0 / total, 0.0)
            summed = jnp.dot(weights.astype(jnp.bfloat16), value_rows, preferred_element_type=jnp.float32)
            o_ref[rows, cols] = (summed * inverse).astype(jnp.bfloat16)
    if moves:
        carry_out.wait()


def attend(queries, kv_slots, block_mask, carried=None):
    tokens, width = queries.shape
    moves = carried is not None
    anywhere = pl.BlockSpec(memory_space=pl.ANY)
    vmem = pl.BlockSpec(memory_space=pltpu.VMEM)
    shapes = [jax.ShapeDtypeStruct((tokens, width), jnp.bfloat16)]
    operands = [block_mask, queries, kv_slots]
    scratch = []
    if moves:
        shapes.append(jax.ShapeDtypeStruct(carried.shape, carried.dtype))
        operands.append(carried)
        scratch += [pltpu.VMEM(carried.shape, carried.dtype), pltpu.SemaphoreType.DMA((2,))]
    return pl.pallas_call(
        functools.partial(attend_kernel, moves),
        out_shape=tuple(shapes),
        in_specs=[pl.BlockSpec(memory_space=pltpu.SMEM), vmem, vmem] + [anywhere] * moves,
        out_specs=tuple([vmem] + [anywhere] * moves),
        scratch_shapes=scratch,
        cost_estimate=pl.CostEstimate(
            flops=4 * tokens * kv_slots.shape[0] * width, bytes_accessed=4 * tokens * width,
            transcendentals=tokens * kv_slots.shape[0] * width // HDIM),
        compiler_params=pltpu.CompilerParams(vmem_limit_bytes=60 * 1024 * 1024),
    )(*operands)


MESH = pl.DeviceIdType.MESH


def exchange_kernel(n_seq, n_tp, image_ref, gain_ref, want_ref, expand_any, shrink_any, proj_any, kvw_any,
                    states_ref, kv_ref,
                    expand_ref, shrink_ref, proj_ref, kvw_ref,
                    pair_out, pair_in, cross_out, cross_in, gathered, other, parts, parts_in, image_cut,
                    shares, chosen, slots,
                    l_s, a_s, a_r, c_s, c_r, b_s, b_r, g_r, up_s, down_s, y_s, x_s, m_r, v_s, v_r, s_s, s_r, f_s, f_r):
    s = lax.axis_index("seq")
    t = lax.axis_index("tp")
    z, y = s // 2, s % 2
    x, c = t // 2, t % 2
    last = n_tp - 1
    core, over, skew = 2 * x + 1 - c, 2 * (1 - x) + c, 2 * (1 - x) + 1 - c
    depth = proj_ref.shape[0] // n_tp
    half = 2 * depth
    cap = want_ref.shape[2]

    barrier = pltpu.get_barrier_semaphore()
    for j in range(1, n_tp):
        pl.semaphore_signal(barrier, inc=1, device_id=(s, lax.rem(t + j, n_tp)), device_id_type=MESH)
    for j in range(1, n_seq):
        pl.semaphore_signal(barrier, inc=1, device_id=(lax.rem(s + j, n_seq), t), device_id_type=MESH)

    def half_rows(h):
        return pl.ds(pl.multiple_of(h * half, 128), half)

    loads = [
        pltpu.make_async_copy(kvw_any, kvw_ref, l_s.at[0]),
        pltpu.make_async_copy(proj_any.at[half_rows(1 - c)], proj_ref.at[half_rows(1 - c)], l_s.at[1]),
        pltpu.make_async_copy(proj_any.at[half_rows(c)], proj_ref.at[half_rows(c)], l_s.at[2]),
        pltpu.make_async_copy(expand_any, expand_ref, l_s.at[3]),
        pltpu.make_async_copy(shrink_any, shrink_ref, l_s.at[4]),
    ]
    for load in loads:
        load.start()

    def remote(src, dst, send, recv, where):
        return pltpu.make_async_remote_copy(src_ref=src, dst_ref=dst, send_sem=send, recv_sem=recv,
                                            device_id=where, device_id_type=MESH)

    def arrive(buf, sem):
        pltpu.make_async_copy(buf, buf, sem).wait()

    sent = []

    def go(copy):
        copy.start()
        sent.append(copy)

    def fold_half(h):
        return jnp.dot(proj_ref[half_rows(h), :], kvw_ref[...], preferred_element_type=jnp.float32)

    loads[0].wait()
    loads[1].wait()
    pair_out[...] = fold_half(1 - c).astype(jnp.bfloat16)
    pl.semaphore_wait(barrier, n_tp + n_seq - 2)
    go(remote(pair_out, pair_in, a_s, a_r, (s, core)))
    loads[2].wait()
    own_fold = fold_half(c)
    arrive(pair_in, a_r)
    own_fold += pair_in[...].astype(jnp.float32)
    for ch in range(2):
        cross_out[ch] = own_fold[ch * depth:(ch + 1) * depth, :].astype(jnp.bfloat16)
    holds = z // 2 == x
    passes = z // 2 != x

    def cross(ch):
        return remote(cross_out.at[ch], cross_in.at[ch], c_s.at[ch], c_r.at[ch], (s, over))

    @pl.when(passes)
    def _():
        for ch in range(2):
            cross(ch).start()

    def place(zl, yy, ch):
        return (zl * 2 + yy) * 2 + ch

    def up(i):
        return remote(gathered.at[i], gathered.at[i], up_s.at[i], g_r.at[i], (s + 2, t))

    def down(i):
        return remote(gathered.at[i], gathered.at[i], down_s.at[i], g_r.at[i], (s - 2, t))

    def across(i):
        return remote(gathered.at[i], gathered.at[i], y_s.at[i], g_r.at[i], (2 * z + 1 - y, t))

    def hand(i, k):
        return remote(gathered.at[i], other.at[k], x_s.at[i], m_r.at[k], (s, core))

    def hand_on(zl, yy, ch):
        @pl.when(zl != c)
        def _():
            hand(place(zl, yy, ch), 2 * yy + ch).start()

    def relay(zl, ch):
        i = place(zl, y, ch)
        zz = 2 * x + zl

        @pl.when(z != zz)
        def _():
            arrive(gathered.at[i], g_r.at[i])

        @pl.when((z >= zz) & (z < last))
        def _():
            up(i).start()

        @pl.when((z <= zz) & (z > 0))
        def _():
            down(i).start()

        across(i).start()
        hand_on(zl, y, ch)

    def y_relay(zl, ch):
        i = place(zl, 1 - y, ch)
        arrive(gathered.at[i], g_r.at[i])
        hand_on(zl, 1 - y, ch)

    first = (z + 2 * (1 - x)) // last
    second = 1 - first

    def begin(ch):
        @pl.when(holds)
        def _():
            arrive(cross_in.at[ch], c_r.at[ch])
            gathered[place(first, y, ch)] = (
                cross_out[ch].astype(jnp.float32) + cross_in[ch].astype(jnp.float32)).astype(jnp.bfloat16)
            relay(first, ch)

    values = image_ref[...].astype(jnp.float32)
    center = values - jnp.mean(values, axis=1, keepdims=True)
    spread = jnp.mean(center * center, axis=1, keepdims=True)
    normed = (center * lax.rsqrt(spread + 1e-05) * gain_ref[...][None, :]).astype(jnp.bfloat16)
    loads[3].wait()
    wide = jnp.dot(normed, expand_ref[...], preferred_element_type=jnp.float32)
    hidden = (0.5 * wide * (1.0 + lax.erf(wide * math.sqrt(0.5)))).astype(jnp.bfloat16)
    begin(0)
    loads[4].wait()
    partial = jnp.dot(hidden, shrink_ref[...], preferred_element_type=jnp.float32)
    for q in range(n_tp):
        parts[q] = partial[:, q * depth:(q + 1) * depth].astype(jnp.bfloat16)
        image_cut[q] = values[:, q * depth:(q + 1) * depth]
    for j in range(1, n_tp):
        peer = lax.rem(t + j, n_tp)
        go(remote(parts.at[peer], parts_in.at[j], b_s.at[j], b_r.at[j], (s, peer)))

    begin(1)

    share = parts[t].astype(jnp.float32)
    for j in range(1, n_tp):
        arrive(parts_in.at[j], b_r.at[j])
        share += parts_in[j].astype(jnp.float32)
    share = (image_cut[t] + share).astype(jnp.bfloat16)
    shares[t] = share
    row_id = lax.broadcasted_iota(jnp.int32, (share.shape[0], cap), 0)
    for d in range(n_seq):
        hot = (row_id == want_ref[0, d:d + 1, :]).astype(jnp.float32).astype(jnp.bfloat16)
        chosen[d] = lax.dot_general(
            hot, share, (((0,), (0,)), ((), ())), preferred_element_type=jnp.float32).astype(jnp.bfloat16)
    slots[t, s] = chosen[s]
    for j in range(1, n_seq):
        peer = lax.rem(s + j, n_seq)
        go(remote(chosen.at[peer], slots.at[t, s], s_s.at[j], s_r.at[s], (peer, t)))
    go(remote(shares.at[t], shares.at[t], v_s.at[1], v_r.at[t], (s, core)))
    go(remote(shares.at[t], shares.at[t], v_s.at[2], v_r.at[t], (s, over)))

    @pl.when(passes)
    def _():
        for ch in range(2):
            relay(first, ch)

    @pl.when(holds)
    def _():
        for ch in range(2):
            relay(second, ch)

    for j in range(1, n_seq):
        peer = lax.rem(s + j, n_seq)
        arrive(slots.at[t, peer], s_r.at[peer])
    go(remote(slots.at[t], slots.at[t], f_s.at[1], f_r.at[t], (s, core)))
    go(remote(slots.at[t], slots.at[t], f_s.at[2], f_r.at[t], (s, over)))
    arrive(shares.at[over], v_r.at[over])
    go(remote(shares.at[over], shares.at[over], v_s.at[3], v_r.at[over], (s, core)))
    for ch in range(2):
        @pl.when(passes)
        def _():
            relay(second, ch)
        y_relay(first, ch)
    arrive(slots.at[over], f_r.at[over])
    go(remote(slots.at[over], slots.at[over], f_s.at[3], f_r.at[over], (s, core)))

    arrive(shares.at[core], v_r.at[core])
    arrive(shares.at[skew], v_r.at[skew])
    n_cut = 4
    cut = states_ref.shape[1] // n_cut
    for n in range(n_cut):
        cols = slice(n * cut, (n + 1) * cut)
        total = None
        for q in range(n_tp):
            term = jnp.dot(shares[q], proj_ref[q * depth:(q + 1) * depth, cols], preferred_element_type=jnp.float32)
            total = term if total is None else total + term
        states_ref[:, cols] = total.astype(jnp.bfloat16)
        if n == 1:
            y_relay(second, 0)

    arrive(slots.at[core], f_r.at[core])
    arrive(slots.at[skew], f_r.at[skew])
    y_relay(second, 1)
    width = kvw_ref.shape[1]
    for yy in range(2):
        total = None
        for ch in range(2):
            rows = slots[2 * c + ch].reshape(n_seq * cap, depth)
            term = jnp.dot(rows, gathered[place(c, yy, ch)], preferred_element_type=jnp.float32)
            total = term if total is None else total + term
        for ch in range(2):
            arrive(other.at[2 * yy + ch], m_r.at[2 * yy + ch])
            rows = slots[2 * (1 - c) + ch].reshape(n_seq * cap, depth)
            total += jnp.dot(rows, other[2 * yy + ch], preferred_element_type=jnp.float32)
        kv_ref[:, yy * width:(yy + 1) * width] = total.astype(jnp.bfloat16)

    for copy in sent:
        copy.wait_send()

    @pl.when(passes)
    def _():
        for ch in range(2):
            cross(ch).wait_send()

    for zl in range(2):
        zz = 2 * x + zl
        for ch in range(2):
            i = place(zl, y, ch)
            across(i).wait_send()

            @pl.when((z >= zz) & (z < last))
            def _():
                up(i).wait_send()

            @pl.when((z <= zz) & (z > 0))
            def _():
                down(i).wait_send()

            @pl.when(zl != c)
            def _():
                for yy in range(2):
                    hand(place(zl, yy, ch), 2 * yy + ch).wait_send()


def exchange(n_seq, n_tp, image_rows, norm_gain, send_list, expand_weight, shrink_weight, projector, kv_weight):
    rows, features = image_rows.shape
    depth = features // n_tp
    width = kv_weight.shape[1]
    cap = send_list.shape[2]
    bf16, f32 = jnp.bfloat16, jnp.float32
    dma = pltpu.SemaphoreType.DMA
    vmem = pl.BlockSpec(memory_space=pltpu.VMEM)
    anywhere = pl.BlockSpec(memory_space=pl.ANY)
    return pl.pallas_call(
        functools.partial(exchange_kernel, n_seq, n_tp),
        out_shape=(jax.ShapeDtypeStruct((rows, projector.shape[1]), bf16),
                   jax.ShapeDtypeStruct((n_seq * cap, 2 * width), bf16)),
        in_specs=[vmem] * 3 + [anywhere] * 4,
        out_specs=(vmem, vmem),
        scratch_shapes=[
            pltpu.VMEM(expand_weight.shape, bf16),
            pltpu.VMEM(shrink_weight.shape, bf16),
            pltpu.VMEM(projector.shape, bf16),
            pltpu.VMEM(kv_weight.shape, bf16),
            pltpu.VMEM((2 * depth, width), bf16),
            pltpu.VMEM((2 * depth, width), bf16),
            pltpu.VMEM((2, depth, width), bf16),
            pltpu.VMEM((2, depth, width), bf16),
            pltpu.VMEM((8, depth, width), bf16),
            pltpu.VMEM((4, depth, width), bf16),
            pltpu.VMEM((n_tp, rows, depth), bf16),
            pltpu.VMEM((n_tp, rows, depth), bf16),
            pltpu.VMEM((n_tp, rows, depth), f32),
            pltpu.VMEM((n_tp, rows, depth), bf16),
            pltpu.VMEM((n_seq, cap, depth), bf16),
            pltpu.VMEM((n_tp, n_seq, cap, depth), bf16),
            dma((5,)), dma, dma, dma((2,)), dma((2,)), dma((n_tp,)), dma((n_tp,)),
            dma((8,)), dma((8,)), dma((8,)), dma((8,)), dma((8,)), dma((4,)),
            dma((n_tp,)), dma((n_tp,)), dma((n_seq,)), dma((n_seq,)), dma((n_tp,)), dma((n_tp,)),
        ],
        compiler_params=pltpu.CompilerParams(
            collective_id=0, has_side_effects=True, vmem_limit_bytes=56 * 1024 * 1024),
    )(image_rows, norm_gain, send_list, expand_weight, shrink_weight, projector, kv_weight)


def local(
    image_rows,
    norm_gain,
    expand_weight,
    shrink_weight,
    projector,
    kv_weight,
    queries,
    send_list,
    block_mask,
):
    wanted = send_list[0]
    n_seq, n_tp = lax.axis_size("seq"), lax.axis_size("tp")
    if n_seq == 8 and n_tp == 4 and kv_weight.shape[1] == 2 * HDIM and wanted.shape[1] % 16 == 0:
        states, kv_slots = exchange(
            n_seq, n_tp, image_rows, norm_gain, send_list, expand_weight, shrink_weight, projector, kv_weight)
        context, states = attend(queries, kv_slots, block_mask, states)
        return (states, context)
    fold_part = jnp.dot(projector, kv_weight, preferred_element_type=jnp.float32).astype(jnp.bfloat16)
    fold_rows = lax.psum_scatter(fold_part, "tp", scatter_dimension=0, tiled=True)
    fold_rows = lax.all_gather(fold_rows, "seq", axis=1, tiled=True)
    normed = layer_norm(image_rows, norm_gain)
    hidden = jax.nn.gelu(
        jnp.dot(normed, expand_weight, preferred_element_type=jnp.float32), approximate=False
    ).astype(jnp.bfloat16)
    partial_value = jnp.dot(hidden, shrink_weight, preferred_element_type=jnp.float32).astype(jnp.bfloat16)
    own_sum = lax.psum_scatter(partial_value, "tp", scatter_dimension=1, tiled=True)
    share_width = own_sum.shape[1]
    own_rows = lax.dynamic_slice_in_dim(
        image_rows, lax.axis_index("tp") * share_width, share_width, 1
    )
    own_share = (own_rows.astype(jnp.float32) + own_sum.astype(jnp.float32)).astype(jnp.bfloat16)
    vit_out = lax.all_gather(own_share, "tp", axis=1, tiled=True)
    states = jnp.dot(vit_out, projector, preferred_element_type=jnp.float32).astype(jnp.bfloat16)
    outgoing = select_rows(own_share, wanted)
    arrived = lax.all_to_all(outgoing, "seq", split_axis=0, concat_axis=0, tiled=True)
    slot_rows = arrived.reshape(-1, share_width)
    kv_part = jnp.dot(slot_rows, fold_rows, preferred_element_type=jnp.float32).astype(jnp.bfloat16)
    kv_slots = lax.psum_scatter(kv_part, "tp", scatter_dimension=1, tiled=True)
    return (states, attend(queries, kv_slots, block_mask)[0])


def solution(mesh):
    placed = (
        P("seq", None),
        P(),
        P(None, "tp"),
        P("tp", None),
        P(None, "tp"),
        P("tp", "seq"),
        P("seq", "tp"),
        P("seq", None, None),
        P("seq", None),
    )
    return jax.shard_map(
        local,
        mesh=mesh,
        in_specs=placed,
        out_specs=(P("seq", "tp"), P("seq", "tp")),
        check_vma=False,
    )
```
